128 devices in a mesh: region: 4 (over z), dev: 32 (over y, x, core).
Axes of the slice: x: 4, y: 4, z: 4, core: 2. Of those that a mesh axis runs over, the one named last changes fastest.
Arguments:
- states: bfloat16 [32768, 512], P(('region', 'dev')), may hold values from -6 to 6
- norm_gain: float32 [512], replicated, may hold values from 0.1 to 1.9
- w_query: bfloat16 [512, 512], replicated, may hold values from -0.25 to 0.25
- w_key: bfloat16 [512, 512], replicated, may hold values from -0.25 to 0.25
- w_value: bfloat16 [512, 512], replicated, may hold values from -1 to 1
- w_out: bfloat16 [512, 512], replicated, may hold values from -0.25 to 0.25
- neighbours: int32 [256, 6], P(('region', 'dev')), may hold values from 0 to 255, as said below
- labels: int32 [256, 128], P(('region', 'dev')), may hold values from 0 to 3
- cotangent: bfloat16 [32768, 512], P(('region', 'dev')), may hold values from -6 to 6
Outputs:
- branch_out: bfloat16 [32768, 512], P(('region', 'dev'))
- grad_states: bfloat16 [32768, 512], P(('region', 'dev'))
- grad_query: float32 [512, 512], replicated
- grad_key: float32 [512, 512], replicated
- grad_value: float32 [512, 512], replicated
- grad_output: float32 [512, 512], replicated
- grad_gain: float32 [512], replicated
The draws below stay inside these ranges and needn't reach their ends.
Inputs may be any that keep to these rules, and one draw needn't show every extreme that they name: `neighbours`: blocks are numbered device by device, region group first, then dev index, 2 to a device. Entry 0 of row b is b itself. Entries 1 to 4 lie on devices of b's own region group; over the 2 blocks of one device these 8 entries name distinct blocks, at most 1 of them on any one device, and exactly 1 on some device. Entry 5 lies in the next region group (the last group's next is the first) at the same dev index, and the entries 5 of one device's blocks name each block of that device once.
All inputs are finite; a program needn't handle non-finite values.
Results may differ from the reference program's by a relative error of at most 0.015.
Values may be sent and summed in bfloat16 or wider, within the bound.
A program may use at most 128 MiB of HBM per device.

```python
import math
import jax
import jax.numpy as jnp
from jax import lax

D = 512
HEADS = 8
BLOCK_ROWS = 128
NEIGHBOURS = 6
BLK_DEV = 2
CAP = 1
BLOCKS = 256
STATES = 32768
N_REGION = 4
N_DEV = 32


def draw_neighbours(key, part):
    slot_count = N_DEV * CAP
    request_count = 4 * BLK_DEV

    def one_device(device_id):
        device_key = jax.random.fold_in(key, device_id)
        key_full, key_rank, key_offset, key_shuffle, key_cross = jax.random.split(device_key, 5)
        region = device_id // N_DEV
        dev_position = device_id % N_DEV
        full_peer = jax.random.randint(key_full, (), 0, N_DEV)
        rankings = jax.random.permutation(key_rank, slot_count)
        slot_ids = jnp.arange(slot_count, dtype=jnp.int32)
        priority = jnp.where(slot_ids // CAP == full_peer, -1, rankings)
        chosen = jnp.argsort(priority, stable=True)[:request_count]
        peers = chosen // CAP
        within = chosen % CAP
        offset = jax.random.randint(key_offset, (N_DEV,), 0, BLK_DEV)
        local_ids = (within + offset[peers]) % BLK_DEV
        inside = (region * N_DEV + peers) * BLK_DEV + local_ids
        shuffle = jax.random.permutation(key_shuffle, request_count)
        inside = inside[shuffle].reshape(BLK_DEV, 4)
        cross_order = jax.random.permutation(key_cross, BLK_DEV)
        across = ((region + 1) % N_REGION * N_DEV + dev_position) * BLK_DEV + cross_order
        itself = device_id * BLK_DEV + jnp.arange(BLK_DEV, dtype=jnp.int32)
        return jnp.concatenate([itself[:, None], inside, across[:, None]], axis=1).astype(jnp.int32)
    listing = jax.vmap(one_device)(jnp.arange(N_REGION * N_DEV, dtype=jnp.int32))
    return listing.reshape(BLOCKS, 6).astype(jnp.int32)


def plant(values, rng, low, largest):
    index_at = [jax.random.randint(jax.random.fold_in(rng, axis), (), 0, length) for axis, length in enumerate(values.shape)]
    main_axis = values.shape.index(max(values.shape))
    neighbour = index_at[:main_axis] + [(index_at[main_axis] + 1) % values.shape[main_axis]] + index_at[main_axis + 1:]
    return values.at[tuple(index_at)].set(low).at[tuple(neighbour)].set(largest)


def block_levels(rng, shape, cuts, least, high):
    gain = 1.0
    for dim, blocks in cuts:
        heights = jax.random.uniform(jax.random.fold_in(jax.random.fold_in(rng, 6), dim), (blocks,), jnp.float32, least / len(cuts), high / len(cuts))
        gain = gain * jnp.repeat(jnp.exp(heights), shape[dim] // blocks).reshape((-1,) + (1,) * (len(shape) - 1 - dim))
    return gain


def scatter_about(stream_key, extent, deviation, reach, pieces=(), held_as=jnp.bfloat16):
    drawn = deviation * jax.random.normal(stream_key, extent, jnp.float32)
    if pieces:
        drawn = drawn * block_levels(stream_key, extent, pieces, -0.22, 0.18)
    return jnp.clip(drawn, -reach, reach).astype(held_as)


def setup_inputs(seed: int = 0) -> dict:
    key_list = jax.random.split(jax.random.key(seed), 10)
    return {
        "states": scatter_about(key_list[0], (STATES, D), 1.0, 6.0, ((0, 128),)),
        "norm_gain": jnp.clip(1.0 + 0.18 * jax.random.normal(key_list[1], (D,), jnp.float32), 0.1, 1.9),
        "w_query": scatter_about(key_list[2], (D, D), D ** -0.5, 0.25),
        "w_key": scatter_about(key_list[3], (D, D), D ** -0.5, 0.25),
        "w_value": scatter_about(key_list[4], (D, D), (D // 16) ** -0.5, 1.0),
        "w_out": scatter_about(key_list[5], (D, D), D ** -0.5, 0.25),
        "neighbours": draw_neighbours(jax.random.fold_in(key_list[9], 71), 0),
        "labels": plant(jax.random.randint(key_list[7], (BLOCKS, BLOCK_ROWS), 0, 4), jax.random.fold_in(key_list[7], 1), 0, 3).astype(jnp.int32),
        "cotangent": scatter_about(key_list[8], (STATES, D), 1.0, 6.0, ((0, 128),)),
    }


EPSILON = 1e-05

def normalize(row_block, norm_gain):
    widened = row_block.astype(jnp.float32)
    inverse = lax.rsqrt(lax.optimization_barrier(jnp.mean(widened * widened, axis=-1, keepdims=True)) + EPSILON)
    return ((widened * inverse * norm_gain).astype(jnp.bfloat16), inverse)

def normalize_back(row_block, norm_gain, inverse, d_normed):
    widened = row_block.astype(jnp.float32)
    grad_gain = lax.optimization_barrier(jnp.sum(d_normed * widened * inverse, axis=0))
    along_rows = lax.optimization_barrier(jnp.sum(d_normed * norm_gain * widened, axis=-1, keepdims=True)) / row_block.shape[-1]
    grad_rows = inverse * norm_gain * d_normed - widened * inverse * inverse * inverse * along_rows
    return (grad_gain, grad_rows.astype(jnp.bfloat16))

def attend(query_block, keyval, allowed):
    model_width = query_block.shape[-1]
    head_dim = model_width // HEADS
    query_count = query_block.shape[0]
    key_pairs = keyval.reshape(-1, 2 * model_width)
    key_count = key_pairs.shape[0]
    query_heads = query_block.astype(jnp.float32).reshape(query_count, HEADS, head_dim)
    key_heads = key_pairs[:, :model_width].astype(jnp.float32).reshape(key_count, HEADS, head_dim)
    value_heads = key_pairs[:, model_width:].astype(jnp.float32).reshape(key_count, HEADS, head_dim)
    scores = jnp.einsum('qhd,khd->hqk', query_heads, key_heads) / math.sqrt(head_dim)
    weights = jnp.where(allowed[None], jnp.exp(scores), 0.0)
    probabilities = (weights / lax.optimization_barrier(jnp.sum(weights, axis=-1, keepdims=True))).astype(jnp.bfloat16)
    mixture = jnp.einsum('hqk,khd->qhd', probabilities.astype(jnp.float32), value_heads)
    return mixture.reshape(query_count, model_width).astype(jnp.bfloat16)

def project(row_block, weight):
    return jnp.dot(row_block, weight, preferred_element_type=jnp.float32).astype(jnp.bfloat16)

def reference(states, norm_gain, w_query, w_key, w_value, w_out, neighbours, labels, cotangent):
    normed, inverse = normalize(states, norm_gain)
    queries = project(normed, w_query)
    key_rows = project(normed, w_key)
    value_rows = project(normed, w_value)
    keyval_all = jnp.concatenate([key_rows, value_rows], axis=-1).reshape(BLOCKS, BLOCK_ROWS, 2 * D)
    normed_blocks = normed.reshape(BLOCKS, BLOCK_ROWS, D)
    query_blocks = queries.reshape(BLOCKS, BLOCK_ROWS, D)
    d_attention = jnp.dot(cotangent, w_out.T, preferred_element_type=jnp.float32).astype(jnp.bfloat16)
    grad_blocks = d_attention.reshape(BLOCKS, BLOCK_ROWS, D)

    def block_step(carried, block_id):
        totals, grad_pairs = carried
        listed = neighbours[block_id]
        keyval = keyval_all[listed]
        key_labels = labels[listed].reshape(-1)
        allowed = jnp.abs(labels[block_id][:, None] - key_labels[None, :]) <= 1

        def local_attention(query_rows, key_pairs):
            return attend(query_rows, key_pairs, allowed)
        mixture, pullback = jax.vjp(local_attention, query_blocks[block_id], keyval)
        d_query, d_pairs = pullback(grad_blocks[block_id])
        pair_rows = d_pairs.astype(jnp.bfloat16).reshape(-1, 2 * D)
        normed_keys = normed_blocks[listed].reshape(-1, D)
        grad_pairs = grad_pairs + jnp.dot(normed_keys.T, pair_rows, preferred_element_type=jnp.float32)
        part = jnp.dot(pair_rows[:, :D], w_key.T, preferred_element_type=jnp.float32)
        part = part + jnp.dot(pair_rows[:, D:], w_value.T, preferred_element_type=jnp.float32)
        part = part.astype(jnp.bfloat16).astype(jnp.float32).reshape(NEIGHBOURS, BLOCK_ROWS, D)
        totals = totals.at[listed].add(part)
        return ((totals, grad_pairs), (mixture, d_query))
    start = (jnp.zeros((BLOCKS, BLOCK_ROWS, D), jnp.float32), jnp.zeros((D, 2 * D), jnp.float32))
    carried, (mixture, d_query) = lax.scan(block_step, start, jnp.arange(BLOCKS, dtype=jnp.int32))
    totals, grad_pairs = carried
    attention = mixture.reshape(STATES, D)
    branch_out = jnp.dot(attention, w_out, preferred_element_type=jnp.float32).astype(jnp.bfloat16)
    d_queries = d_query.reshape(STATES, D)
    grad_scale = 1.0 / math.sqrt(STATES)
    grad_query = jnp.dot(normed.T, d_queries, preferred_element_type=jnp.float32) * grad_scale
    grad_key = grad_pairs[:, :D] * grad_scale
    grad_value = grad_pairs[:, D:] * grad_scale
    grad_output = jnp.dot(attention.T, cotangent, preferred_element_type=jnp.float32) * grad_scale
    d_normed = jnp.dot(d_queries, w_query.T, preferred_element_type=jnp.float32)
    d_normed = d_normed + totals.reshape(STATES, D)
    grad_gain, grad_states = normalize_back(states, norm_gain, inverse, d_normed)
    return (branch_out, grad_states, grad_query, grad_key, grad_value, grad_output, grad_gain * grad_scale)
```

```python
import math

import jax
import jax.numpy as jnp
from jax import lax
from jax.experimental import pallas as pl
from jax.experimental.pallas import tpu as pltpu
from jax.sharding import PartitionSpec as P

MESH = pl.DeviceIdType.MESH
HEADS = 8
EPSILON = 1e-05
F32 = jnp.float32
BF16 = jnp.bfloat16
VMEM_LIMIT = 56 * 1024 * 1024
NN = (((1,), (0,)), ((), ()))
NT = (((1,), (1,)), ((), ()))
TN = (((0,), (0,)), ((), ()))


def dot(left, right, how=NN):
    return lax.dot_general(left, right, how, preferred_element_type=F32)


def place():
    r = lax.axis_index("region")
    d = lax.axis_index("dev")
    c = lax.rem(d, 2)
    x = lax.rem(lax.div(d, 2), 4)
    y = lax.div(d, 8)
    return r, c, x * (1 - c) + y * c, y * (1 - c) + x * c


def turn(value, step):
    return lax.rem(value + step + 4, 4)


def dev_at(a, b, c):
    return ((b * (1 - c) + a * c) * 4 + a * (1 - c) + b * c) * 2 + c


def around(value):
    return [value, turn(value, -1), turn(value, 1), turn(value, 2)]


def gather_kernel(states, labels, g, gl, far, fl, ssem, rsem, csend, crecv, lsem, lrsem, zsem, zrsem, own_sem):
    r, c, a, b = place()
    def to_dev(dev):
        return (r, dev)
    ap, am = to_dev(dev_at(turn(a, 1), b, c)), to_dev(dev_at(turn(a, -1), b, c))
    bp, bm = to_dev(dev_at(a, turn(b, 1), c)), to_dev(dev_at(a, turn(b, -1), c))
    mate = to_dev(lax.axis_index("dev") + 1 - 2 * c)
    zm, zp = (turn(r, -1), lax.axis_index("dev")), (turn(r, 1), lax.axis_index("dev"))
    barrier = pltpu.get_barrier_semaphore()
    for n in (ap, am, bp, bm, mate, zm, zp):
        pl.semaphore_signal(barrier, inc=1, device_id=n, device_id_type=MESH)
    pl.semaphore_wait(barrier, 7)
    started = []
    def send(src, dst, dev, s, q):
        copy = pltpu.make_async_remote_copy(src_ref=src, dst_ref=dst, send_sem=s, recv_sem=q, device_id=dev, device_id_type=MESH)
        copy.start()
        started.append(copy)
    def got(dst, s, q):
        pltpu.make_async_remote_copy(src_ref=dst, dst_ref=dst, send_sem=s, recv_sem=q, device_id=mate, device_id_type=MESH).wait_recv()
    lo, hi = pl.ds(0, 128), pl.ds(128, 128)
    ak = [a, turn(a, -1), turn(a, 1), turn(a, 2)]
    bk = [b, turn(b, -1), turn(b, 1), turn(b, 2)]
    def slot(i, j):
        return g.at[c, bk[j], ak[i]]
    def oslot(i, j):
        return g.at[1 - c, bk[j], ak[i]]
    def run(index, src, dst, dev):
        send(src, dst, dev, ssem.at[index], rsem.at[index])
    def arrived(index, dst):
        got(dst, ssem.at[index], rsem.at[index])
    def cross(i, j):
        src = states if i == 0 and j == 0 else slot(i, j)
        send(src, slot(i, j), mate, csend.at[i * 4 + j], crecv.at[i * 4 + j])
    run(0, states, slot(0, 0), ap)
    run(1, states, slot(0, 0), am)
    run(4, states, slot(0, 0), bp)
    run(5, states, slot(0, 0), bm)
    send(states, far, zm, zsem.at[0], zrsem.at[0])
    send(labels, fl, zm, zsem.at[1], zrsem.at[1])
    lrow = gl.at[c, b, a]
    send(labels, lrow, ap, lsem.at[0], lrsem.at[0])
    send(labels, lrow, am, lsem.at[1], lrsem.at[1])
    cross(0, 0)
    own = [pltpu.make_async_copy(states, slot(0, 0), own_sem.at[0]), pltpu.make_async_copy(labels, lrow, own_sem.at[1])]
    for o in own:
        o.start()
    got(gl.at[c, b, ak[1]], lsem.at[0], lrsem.at[0])
    send(gl.at[c, b, ak[1]], gl.at[c, b, ak[1]], ap, lsem.at[2], lrsem.at[2])
    got(gl.at[c, b, ak[2]], lsem.at[1], lrsem.at[1])
    arrived(0, slot(1, 0))
    run(2, slot(1, 0).at[lo], slot(1, 0).at[lo], ap)
    run(8, slot(1, 0), slot(1, 0), bp)
    run(9, slot(1, 0), slot(1, 0), bm)
    cross(1, 0)
    arrived(1, slot(2, 0))
    run(3, slot(2, 0).at[hi], slot(2, 0).at[hi], am)
    run(12, slot(2, 0), slot(2, 0), bp)
    run(13, slot(2, 0), slot(2, 0), bm)
    cross(2, 0)
    for o in own:
        o.wait()
    got(gl.at[c, b, ak[3]], lsem.at[2], lrsem.at[2])
    lline = gl.at[c, b]
    send(lline, lline, bp, lsem.at[3], lrsem.at[3])
    send(lline, lline, bm, lsem.at[4], lrsem.at[4])
    def second(i):
        base = 4 + 4 * i
        arrived(base, slot(i, 1))
        run(base + 2, slot(i, 1).at[lo], slot(i, 1).at[lo], bp)
        cross(i, 1)
        arrived(base + 1, slot(i, 2))
        run(base + 3, slot(i, 2).at[hi], slot(i, 2).at[hi], bm)
        cross(i, 2)
    second(0)
    arrived(2, slot(3, 0).at[lo])
    arrived(3, slot(3, 0).at[hi])
    run(16, slot(3, 0), slot(3, 0), bp)
    run(17, slot(3, 0), slot(3, 0), bm)
    cross(3, 0)
    got(gl.at[c, bk[1]], lsem.at[3], lrsem.at[3])
    send(gl.at[c, bk[1]], gl.at[c, bk[1]], bp, lsem.at[5], lrsem.at[5])
    got(gl.at[c, bk[2]], lsem.at[4], lrsem.at[4])
    second(1)
    second(2)
    second(3)
    got(gl.at[c, bk[3]], lsem.at[5], lrsem.at[5])
    send(gl.at[c], gl.at[c], mate, lsem.at[6], lrsem.at[6])
    for i in range(4):
        base = 4 + 4 * i
        arrived(base + 2, slot(i, 3).at[lo])
        arrived(base + 3, slot(i, 3).at[hi])
        cross(i, 3)
    for i in range(4):
        for j in range(4):
            pltpu.make_async_remote_copy(src_ref=states, dst_ref=g.at[1 - c, ak[j], bk[i]], send_sem=csend.at[i * 4 + j], recv_sem=crecv.at[i * 4 + j], device_id=mate, device_id_type=MESH).wait_recv()
    got(gl.at[1 - c], lsem.at[6], lrsem.at[6])
    got(far, zsem.at[0], zrsem.at[0])
    got(fl, zsem.at[1], zrsem.at[1])
    for s in started:
        s.wait_send()

def gather(states, labels):
    dma = pltpu.SemaphoreType.DMA
    return pl.pallas_call(
        gather_kernel,
        out_shape=(
            jax.ShapeDtypeStruct((2, 4, 4, 256, 512), jnp.bfloat16),
            jax.ShapeDtypeStruct((2, 4, 4, 2, 128), jnp.int32),
            jax.ShapeDtypeStruct((256, 512), jnp.bfloat16),
            jax.ShapeDtypeStruct((2, 128), jnp.int32),
        ),
        in_specs=[pl.BlockSpec(memory_space=pl.ANY)] * 2,
        out_specs=[pl.BlockSpec(memory_space=pl.ANY)] * 4,
        scratch_shapes=[dma((20,)), dma((20,)), dma((16,)), dma((16,)), dma((7,)), dma((7,)), dma((2,)), dma((2,)), dma((2,))],
        compiler_params=pltpu.CompilerParams(collective_id=0, has_side_effects=True),
    )(states, labels)


def normalize(rows, gain):
    wide = rows.astype(F32)
    inverse = lax.rsqrt(jnp.mean(wide * wide, axis=-1, keepdims=True) + EPSILON)
    return (wide * inverse * gain).astype(BF16)


def attend_kernel(
    near_ref, states, gain, wq, wk, wv, wo, labels, cot, g, gl, far, fl,
    branch, parts, far_parts, base_t, grads, table,
    fetched, normed, q_own, d_att, keys, normed_keys, values, key_marks, bias,
    q_wide, d_wide, scores, d_probs, probs, d_scores, att, dq, kv_grad, kv_sum, sems,
):
    copies = []
    for b in range(2):
        for e in range(4):
            n = near_ref[b, 1 + e]
            dev = lax.rem(lax.div(n, 2), 32)
            c = lax.rem(dev, 2)
            x = lax.rem(lax.div(dev, 2), 4)
            y = lax.div(dev, 8)
            slot = c * 16 + (y * (1 - c) + x * c) * 4 + x * (1 - c) + y * c
            local = lax.rem(n, 2)
            copy = pltpu.make_async_copy(
                g.at[slot, pl.ds(pl.multiple_of(local * 128, 128), 128)],
                fetched.at[b * 4 + e], sems.at[b * 4 + e])
            copy.start()
            copies.append(copy)
            key_marks[b, :, (1 + e) * 128 : (2 + e) * 128] = jnp.broadcast_to(gl[slot, pl.ds(local, 1)], (8, 128)).astype(F32)

    def clear(k, _):
        table[k] = 8
        return 0

    lax.fori_loop(0, 64, clear, 0)
    for b in range(2):
        for e in range(4):
            table[lax.rem(near_ref[b, 1 + e], 64)] = b * 4 + e
    parts[8] = jnp.zeros((512, 128), BF16)
    gain_row = gain[...]
    for b in range(2):
        rows = slice(b * 128, (b + 1) * 128)
        normed[rows] = normalize(states[rows], gain_row)
        q_own[rows] = (dot(normed[rows], wq[...]) .astype(BF16) * 0.125).astype(BF16)
        d_att[rows] = dot(cot[rows], wo[...], NT).astype(BF16)
        normed_keys[b, :128] = normed[rows]
        m = lax.rem(near_ref[b, 5], 2)
        normed_keys[b, 640:] = normalize(far[pl.ds(pl.multiple_of(m * 128, 128), 128)], gain_row)
        key_marks[b, :, :128] = jnp.broadcast_to(labels[b : b + 1], (8, 128)).astype(F32)
        key_marks[b, :, 640:] = jnp.broadcast_to(fl[pl.ds(m, 1)], (8, 128)).astype(F32)
    for b in range(2):
        for e in range(4):
            copies[b * 4 + e].wait()
            normed_keys[b, (1 + e) * 128 : (2 + e) * 128] = normalize(fetched[b * 4 + e], gain_row)

    def project(k, _):
        b, e = lax.div(k, 6), lax.rem(k, 6)
        rows = pl.ds(pl.multiple_of(e * 128, 128), 128)
        n = normed_keys[b, rows]
        keys[b, rows] = dot(n, wk[...]).astype(BF16)
        values[b, rows] = dot(n, wv[...]).astype(BF16)
        return 0

    lax.fori_loop(0, 12, project, 0)
    head_of = lax.broadcasted_iota(jnp.int32, (128, 256), 1) // 64
    for b in range(2):
        rows = slice(b * 128, (b + 1) * 128)
        own = jnp.broadcast_to(labels[b : b + 1], (128, 128)).astype(F32).T
        for e in range(6):
            at = slice(e * 128, (e + 1) * 128)
            gap = jnp.abs(own - jnp.broadcast_to(key_marks[b, :1, at], (128, 128)))
            bias[:, at] = jnp.where(gap <= 1.0, 0.0, -jnp.inf)
        for half in range(2):
            cols = slice(half * 256, (half + 1) * 256)
            for i in range(4):
                at = slice(i * 128, (i + 1) * 128)
                q_wide[at] = jnp.where(head_of == i, q_own[rows, cols].astype(F32), 0.0).astype(BF16)
                d_wide[at] = jnp.where(head_of == i, d_att[rows, cols].astype(F32), 0.0).astype(BF16)
            scores[...] = dot(q_wide[...], keys[b, :, cols], NT)
            d_probs[...] = dot(d_wide[...], values[b, :, cols], NT)

            def soft(k, _):
                at = pl.ds(pl.multiple_of(k * 32, 32), 32)
                bt = pl.ds(pl.multiple_of(lax.rem(k, 4) * 32, 32), 32)
                w = jnp.exp(scores[at] + bias[bt])
                p = w * (1.0 / jnp.sum(w, axis=-1, keepdims=True))
                dp = d_probs[at]
                mean = jnp.sum(p * dp, axis=-1, keepdims=True)
                probs[at] = p.astype(BF16)
                d_scores[at] = (p * (dp - mean)).astype(BF16)
                return 0

            lax.fori_loop(0, 16, soft, 0)
            mixed = dot(probs[...], values[b, :, cols])
            turned = dot(d_scores[...], keys[b, :, cols])
            one = jnp.zeros((128, 256), F32)
            two = jnp.zeros((128, 256), F32)
            for i in range(4):
                at = slice(i * 128, (i + 1) * 128)
                one = one + jnp.where(head_of == i, mixed[at], 0.0)
                two = two + jnp.where(head_of == i, turned[at], 0.0)
            att[rows, cols] = one.astype(BF16)
            dq[rows, cols] = (two * 0.125).astype(BF16)
            kv_grad[b, cols] = dot(q_wide[...], d_scores[...], TN).astype(BF16)
            kv_grad[b, 512 + half * 256 : 768 + half * 256] = dot(d_wide[...], probs[...], TN).astype(BF16)
    branch[...] = dot(att[...], wo[...]).astype(BF16)
    grads[:512] = dot(normed[...], dq[...], TN).astype(BF16)
    grads[1536:] = dot(att[...], cot[...], TN).astype(BF16)
    mine = dot(wq[...], dq[...], NT)
    for b in range(2):
        for e in range(6):
            at = slice(e * 128, (e + 1) * 128)
            part = (dot(wk[...], kv_grad[b, :512, at]) + dot(wv[...], kv_grad[b, 512:, at])).astype(BF16)
            if e == 0:
                base_t[:, b * 128 : (b + 1) * 128] = mine[:, b * 128 : (b + 1) * 128] + part.astype(F32)
            elif e < 5:
                parts[b * 4 + e - 1] = part
            else:
                far_parts[lax.rem(near_ref[b, 5], 2)] = part
    for half in range(2):
        at = slice(half * 512, (half + 1) * 512)
        kv_sum[at] = dot(kv_grad[0, at], normed_keys[0]) + dot(kv_grad[1, at], normed_keys[1])
        grads[512 + half * 512 : 1024 + half * 512] = kv_sum[at].T.astype(BF16)


def attend(neighbours, states, gain, wq, wk, wv, wo, labels, cot, g, gl, far, fl):
    vmem = pl.BlockSpec(memory_space=pltpu.VMEM)
    smem = pl.BlockSpec(memory_space=pltpu.SMEM)
    anywhere = pl.BlockSpec(memory_space=pl.ANY)
    return pl.pallas_call(
        attend_kernel,
        out_shape=(
            jax.ShapeDtypeStruct((256, 512), BF16),
            jax.ShapeDtypeStruct((9, 512, 128), BF16),
            jax.ShapeDtypeStruct((2, 512, 128), BF16),
            jax.ShapeDtypeStruct((512, 256), F32),
            jax.ShapeDtypeStruct((2048, 512), BF16),
            jax.ShapeDtypeStruct((64,), jnp.int32),
        ),
        in_specs=[smem] + [vmem] * 8 + [anywhere] + [vmem] * 3,
        out_specs=[vmem] * 5 + [smem],
        scratch_shapes=[
            pltpu.VMEM((8, 128, 512), BF16),
            pltpu.VMEM((256, 512), BF16),
            pltpu.VMEM((256, 512), BF16),
            pltpu.VMEM((256, 512), BF16),
            pltpu.VMEM((2, 768, 512), BF16),
            pltpu.VMEM((2, 768, 512), BF16),
            pltpu.VMEM((2, 768, 512), BF16),
            pltpu.VMEM((2, 8, 768), F32),
            pltpu.VMEM((128, 768), F32),
            pltpu.VMEM((512, 256), BF16),
            pltpu.VMEM((512, 256), BF16),
            pltpu.VMEM((512, 768), F32),
            pltpu.VMEM((512, 768), F32),
            pltpu.VMEM((512, 768), BF16),
            pltpu.VMEM((512, 768), BF16),
            pltpu.VMEM((256, 512), BF16),
            pltpu.VMEM((256, 512), BF16),
            pltpu.VMEM((2, 1024, 768), BF16),
            pltpu.VMEM((1024, 512), F32),
            pltpu.SemaphoreType.DMA((8,)),
        ],
        compiler_params=pltpu.CompilerParams(vmem_limit_bytes=VMEM_LIMIT),
    )(neighbours, states, gain, wq, wk, wv, wo, labels, cot, g, gl, far, fl)


def scatter_kernel(
    table, parts, far_parts, base_t, grads, states, gain,
    grad_states, summed,
    give, take, far_send, far_recv, near_send, near_recv, line,
    far2_recv, near2_send, near2_recv, z_part, total,
    g_mate, g_half, gz_far, gz_near_send, gz_near, gy_own, gy_recv, gx_own, gx_recv,
    give_s, take_s, s1s, s1r, s2s, s2r, zs, zr, gs, gr,
):
    r, c, a, b = place()
    d = lax.axis_index("dev")
    x, y = lax.rem(lax.div(d, 2), 4), lax.div(d, 8)
    ak, bk = around(a), around(b)
    xk, yk, rk = around(x), around(y), around(r)
    mate = (r, d + 1 - 2 * c)
    a_to = [(r, dev_at(k, b, c)) for k in ak]
    b_to = [(r, dev_at(a, k, c)) for k in bk]
    x_to = [(r, (y * 4 + k) * 2 + c) for k in xk]
    y_to = [(r, (k * 4 + x) * 2 + c) for k in yk]
    z_to = [(k, d) for k in rk]
    barrier = pltpu.get_barrier_semaphore()
    peers = [mate] + x_to[1:] + y_to[1:] + z_to[1:3]
    for peer in peers:
        pl.semaphore_signal(barrier, inc=1, device_id=peer, device_id_type=MESH)
    pl.semaphore_wait(barrier, len(peers))
    started = []

    def send(src, dst, s, q, to):
        copy = pltpu.make_async_remote_copy(
            src_ref=src, dst_ref=dst, send_sem=s, recv_sem=q, device_id=to, device_id_type=MESH)
        copy.start()
        started.append(copy)

    def got(dst, s, q):
        pltpu.make_async_remote_copy(
            src_ref=dst, dst_ref=dst, send_sem=s, recv_sem=q, device_id=mate, device_id_type=MESH).wait_recv()

    mate_rows = pl.ds(pl.multiple_of((1 - c) * 1024, 1024), 1024)
    send(grads.at[mate_rows], g_mate, gs.at[0], gr.at[0], mate)
    send(far_parts, z_part, zs.at[0], zr.at[0], z_to[2])

    def fill(dev, into):
        for block in range(2):
            into[block] = parts[table[2 * dev + block]]

    order = (3, 1, 2, 0)
    for j in (3, 1, 2, 0):
        for i in order:
            k = i * 4 + j
            fill(dev_at(bk[i], ak[j], 1 - c), give.at[k])
            send(give.at[k], take.at[k], give_s.at[k], take_s.at[k], mate)

    def here(i, j, block, rows):
        k = i * 4 + j
        mine = parts[table[2 * dev_at(ak[i], bk[j], c) + block], rows]
        return mine.astype(F32) + take[k, block, rows].astype(F32)

    def each(body):
        def step(t, _):
            body(pl.ds(pl.multiple_of(t * 128, 128), 128))
            return 0

        lax.fori_loop(0, 4, step, 0)

    def took(i, j):
        got(take.at[i * 4 + j], give_s.at[i * 4 + j], take_s.at[i * 4 + j])

    got(g_mate, gs.at[0], gr.at[0])
    base = c * 1024

    def half_sum(t, _):
        rows = pl.ds(pl.multiple_of(t * 64, 64), 64)
        from_rows = pl.ds(pl.multiple_of(base + t * 64, 64), 64)
        g_half[rows] = (grads[from_rows].astype(F32) + g_mate[rows].astype(F32)).astype(BF16)
        return 0

    lax.fori_loop(0, 16, half_sum, 0)

    def z_rows(k, offset, size):
        return pl.ds(pl.multiple_of(rk[k] * 256 + offset, 16), size)

    send(g_half.at[z_rows(3, 0, 128)], gz_far.at[0], gs.at[1], gr.at[1], z_to[2])
    send(g_half.at[z_rows(3, 128, 128)], gz_far.at[1], gs.at[2], gr.at[2], z_to[1])

    for i in order:
        took(i, 3)
        for block in range(2):
            def far_sum(rows, block=block, i=i):
                far_send[i, block, rows] = here(i, 3, block, rows).astype(BF16)
            each(far_sum)
            send(far_send.at[i, block], far_recv.at[i, block], s1s.at[i * 4 + block], s1r.at[i * 4 + block], b_to[2 - block])

    for way in range(2):
        k = 2 - way
        got(gz_far.at[way], gs.at[1 + way], gr.at[1 + way])

        def z_near(t, _, way=way, k=k):
            rows = pl.ds(pl.multiple_of(t * 64, 64), 64)
            gz_near_send[way, rows] = g_half[z_rows(k, t * 64, 64)]
            return 0

        lax.fori_loop(0, 4, z_near, 0)
        both = slice(way * 128, way * 128 + 128)
        gz_near_send[way, both] = (gz_near_send[way, both].astype(F32) + gz_far[way].astype(F32)).astype(BF16)
        send(gz_near_send.at[way], gz_near.at[way], gs.at[3 + way], gr.at[3 + way], z_to[k])

    for i in order:
        for way in range(2):
            j = 2 - way
            took(i, j)
            got(far_recv.at[i, way], s1s.at[i * 4 + way], s1r.at[i * 4 + way])

            def near_sum(rows, way=way, i=i, j=j):
                near_send[i, way, way, rows] = (here(i, j, way, rows) + far_recv[i, way, rows].astype(F32)).astype(BF16)
                near_send[i, way, 1 - way, rows] = here(i, j, 1 - way, rows).astype(BF16)
            each(near_sum)
            send(near_send.at[i, way], near_recv.at[i, way], s1s.at[i * 4 + 2 + way], s1r.at[i * 4 + 2 + way], b_to[j])

    for way in range(2):
        got(gz_near.at[way], gs.at[3 + way], gr.at[3 + way])
    gy_own[...] = (g_half[z_rows(0, 0, 256)].astype(F32) + gz_near[0].astype(F32) + gz_near[1].astype(F32)).astype(BF16)

    def small(k, size, pos):
        return pl.ds(pl.multiple_of(pos[k] * size, 16), size)

    for k in range(1, 4):
        send(gy_own.at[small(k, 64, yk)], gy_recv.at[k - 1], gs.at[4 + k], gr.at[4 + k], y_to[k])

    def ring_end(i):
        took(i, 0)
        for way in range(2):
            got(near_recv.at[i, way], s1s.at[i * 4 + 2 + way], s1r.at[i * 4 + 2 + way])
        for block in range(2):
            def end(rows, block=block):
                line[i, block, rows] = (
                    here(i, 0, block, rows) + near_recv[i, 0, block, rows].astype(F32)
                    + near_recv[i, 1, block, rows].astype(F32)).astype(BF16)
            each(end)

    ring_end(3)
    for block in range(2):
        send(line.at[3, block], far2_recv.at[block], s2s.at[block], s2r.at[block], a_to[2 - block])
    ring_end(1)

    for k in range(1, 4):
        got(gy_recv.at[k - 1], gs.at[4 + k], gr.at[4 + k])
    gx_own[...] = (gy_own[small(0, 64, yk)].astype(F32) + gy_recv[0].astype(F32) + gy_recv[1].astype(F32) + gy_recv[2].astype(F32)).astype(BF16)
    for k in range(1, 4):
        send(gx_own.at[small(k, 16, xk)], gx_recv.at[k - 1], gs.at[7 + k], gr.at[7 + k], x_to[k])

    ring_end(2)
    for way in range(2):
        got(far2_recv.at[way], s2s.at[way], s2r.at[way])

        def near2(rows, way=way):
            near2_send[way, way, rows] = (line[2 - way, way, rows].astype(F32) + far2_recv[way, rows].astype(F32)).astype(BF16)
            near2_send[way, 1 - way, rows] = line[2 - way, 1 - way, rows]
        each(near2)
        send(near2_send.at[way], near2_recv.at[way], s2s.at[2 + way], s2r.at[2 + way], a_to[2 - way])

    for k in range(1, 4):
        got(gx_recv.at[k - 1], gs.at[7 + k], gr.at[7 + k])
    start = c * 1024 + r * 256 + y * 64 + x * 16

    def span(first, size):
        return pl.ds(pl.multiple_of(first, 16), size)

    summed[span(start, 16)] = (
        gx_own[small(0, 16, xk)].astype(F32) + gx_recv[0].astype(F32) + gx_recv[1].astype(F32) + gx_recv[2].astype(F32)).astype(BF16)

    def spread(pos, size, first, sem, to):
        for k in range(1, 4):
            send(summed.at[span(first + pos[0] * size, size)], summed.at[span(first + pos[0] * size, size)], gs.at[sem + k], gr.at[sem + k], to[k])

    def spread_in(pos, size, first, sem):
        for k in range(1, 4):
            source = pos[{1: 2, 2: 1, 3: 3}[k]]
            got(summed.at[span(first + source * size, size)], gs.at[sem + k], gr.at[sem + k])

    first_x = c * 1024 + r * 256 + y * 64
    spread(xk, 16, first_x, 10, x_to)
    ring_end(0)
    spread_in(xk, 16, first_x, 10)
    first_y = c * 1024 + r * 256
    spread(yk, 64, first_y, 13, y_to)
    spread_in(yk, 64, first_y, 13)
    first_z = c * 1024
    mine = summed.at[span(first_z + r * 256, 256)]
    send(mine, mine, gs.at[17], gr.at[17], z_to[1])
    send(mine, mine, gs.at[18], gr.at[18], z_to[2])

    for way in range(2):
        got(near2_recv.at[way], s2s.at[2 + way], s2r.at[2 + way])
    got(z_part, zs.at[0], zr.at[0])
    for block in range(2):
        def last(rows, block=block):
            at = slice(block * 128, block * 128 + 128)
            total[rows, at] = (
                base_t[rows, at] + line[0, block, rows].astype(F32) + near2_recv[0, block, rows].astype(F32)
                + near2_recv[1, block, rows].astype(F32) + z_part[block, rows].astype(F32))
        each(last)

    up, down = rk[1], rk[2]
    came_down = summed.at[span(first_z + down * 256, 256)]
    got(came_down, gs.at[17], gr.at[17])
    one = summed.at[span(first_z + down * 256, 128)]
    send(one, one, gs.at[19], gr.at[19], z_to[1])
    came_up = summed.at[span(first_z + up * 256, 256)]
    got(came_up, gs.at[18], gr.at[18])
    two = summed.at[span(first_z + up * 256 + 128, 128)]
    send(two, two, gs.at[20], gr.at[20], z_to[2])

    def finish(t, _):
        rows = pl.ds(pl.multiple_of(t * 128, 128), 128)
        d_normed = total[:, rows].T
        wide = states[rows].astype(F32)
        inverse = lax.rsqrt(jnp.mean(wide * wide, axis=-1, keepdims=True) + EPSILON)
        scaled = d_normed * gain[...]
        along = jnp.sum(scaled * wide, axis=-1, keepdims=True) * (1.0 / 512)
        grad_states[rows] = (inverse * scaled - wide * (inverse * inverse * inverse * along)).astype(BF16)
        return 0

    lax.fori_loop(0, 2, finish, 0)
    got(summed.at[span(first_z + rk[3] * 256, 128)], gs.at[19], gr.at[19])
    got(summed.at[span(first_z + rk[3] * 256 + 128, 128)], gs.at[20], gr.at[20])
    half = summed.at[span(first_z, 1024)]
    send(half, half, gs.at[21], gr.at[21], mate)
    got(summed.at[span(1024 - first_z, 1024)], gs.at[21], gr.at[21])
    for copy in started:
        copy.wait_send()


def scatter(table, parts, far_parts, base_t, grads, states, gain):
    vmem = pl.BlockSpec(memory_space=pltpu.VMEM)
    smem = pl.BlockSpec(memory_space=pltpu.SMEM)
    dma = pltpu.SemaphoreType.DMA
    return pl.pallas_call(
        scatter_kernel,
        out_shape=(jax.ShapeDtypeStruct((256, 512), BF16), jax.ShapeDtypeStruct((2048, 512), BF16)),
        in_specs=[smem] + [vmem] * 6,
        out_specs=[vmem] * 2,
        scratch_shapes=[
            pltpu.VMEM((16, 2, 512, 128), BF16),
            pltpu.VMEM((16, 2, 512, 128), BF16),
            pltpu.VMEM((4, 2, 512, 128), BF16),
            pltpu.VMEM((4, 2, 512, 128), BF16),
            pltpu.VMEM((4, 2, 2, 512, 128), BF16),
            pltpu.VMEM((4, 2, 2, 512, 128), BF16),
            pltpu.VMEM((4, 2, 512, 128), BF16),
            pltpu.VMEM((2, 512, 128), BF16),
            pltpu.VMEM((2, 2, 512, 128), BF16),
            pltpu.VMEM((2, 2, 512, 128), BF16),
            pltpu.VMEM((2, 512, 128), BF16),
            pltpu.VMEM((512, 256), F32),
            pltpu.VMEM((1024, 512), BF16),
            pltpu.VMEM((1024, 512), BF16),
            pltpu.VMEM((2, 128, 512), BF16),
            pltpu.VMEM((2, 256, 512), BF16),
            pltpu.VMEM((2, 256, 512), BF16),
            pltpu.VMEM((256, 512), BF16),
            pltpu.VMEM((3, 64, 512), BF16),
            pltpu.VMEM((64, 512), BF16),
            pltpu.VMEM((3, 16, 512), BF16),
            dma((16,)), dma((16,)), dma((16,)), dma((16,)), dma((4,)), dma((4,)), dma((1,)), dma((1,)),
            dma((22,)), dma((22,)),
        ],
        compiler_params=pltpu.CompilerParams(collective_id=1, has_side_effects=True, vmem_limit_bytes=VMEM_LIMIT),
    )(table, parts, far_parts, base_t, grads, states, gain)


def body(states, norm_gain, w_query, w_key, w_value, w_out, neighbours, labels, cotangent):
    gain = norm_gain.reshape(1, -1)
    g, gl, far, fl = gather(states, labels)
    branch_out, parts, far_parts, base_t, grads, table = attend(
        neighbours, states, gain, w_query, w_key, w_value, w_out, labels, cotangent,
        g.reshape(32, 256, 512), gl.reshape(32, 2, 128), far, fl)
    grad_states, summed = scatter(table, parts, far_parts, base_t, grads, states, gain)
    scale = 1.0 / math.sqrt(32768)
    full = summed.astype(F32).reshape(4, 512, 512) * scale
    along = (
        full[0] * w_query.astype(F32) + full[1] * w_key.astype(F32) + full[2] * w_value.astype(F32))
    grad_gain = jnp.sum(along, axis=1) / norm_gain
    return branch_out, grad_states, full[0], full[1], full[2], full[3], grad_gain


def solution(mesh):
    rows = P(("region", "dev"), None)
    return jax.shard_map(
        body, mesh=mesh,
        in_specs=(rows, P(), P(), P(), P(), P(), rows, rows, rows),
        out_specs=(rows, rows, P(), P(), P(), P(), P()),
        check_vma=False)
```

```python
import math

import jax
import jax.numpy as jnp
from jax import lax
from jax.experimental import pallas as pl
from jax.experimental.pallas import tpu as pltpu
from jax.sharding import PartitionSpec as P

MESH = pl.DeviceIdType.MESH
HEADS = 8
EPSILON = 1e-05
F32 = jnp.float32
BF16 = jnp.bfloat16
VMEM_LIMIT = 56 * 1024 * 1024
NN = (((1,), (0,)), ((), ()))
NT = (((1,), (1,)), ((), ()))
TN = (((0,), (0,)), ((), ()))


def dot(left, right, how=NN):
    return lax.dot_general(left, right, how, preferred_element_type=F32)


def place():
    r = lax.axis_index("region")
    d = lax.axis_index("dev")
    c = lax.rem(d, 2)
    x = lax.rem(lax.div(d, 2), 4)
    y = lax.div(d, 8)
    return r, c, x * (1 - c) + y * c, y * (1 - c) + x * c


def turn(value, step):
    return lax.rem(value + step + 4, 4)


def dev_at(a, b, c):
    return ((b * (1 - c) + a * c) * 4 + a * (1 - c) + b * c) * 2 + c


def around(value):
    return [value, turn(value, -1), turn(value, 1), turn(value, 2)]


def normalize(rows, gain):
    wide = rows.astype(F32)
    inverse = lax.rsqrt(jnp.mean(wide * wide, axis=-1, keepdims=True) + EPSILON)
    return (wide * inverse * gain).astype(BF16)


def remote(src, dst, s, q, to):
    return pltpu.make_async_remote_copy(
        src_ref=src, dst_ref=dst, send_sem=s, recv_sem=q, device_id=to, device_id_type=MESH)


def span(first, size):
    return pl.ds(pl.multiple_of(first, 16), size)


def layer_kernel(
    near_ref, states, gain, labels, wq_hbm, wk_hbm, wv_hbm, wo_hbm, cot_hbm,
    branch, grad_states, summed,
    wq, wk, wv, wo, cot, marks, g, gl, far, fl, table,
    normed, q_own, d_att, keys, normed_keys, values, key_marks, bias,
    q_wide, d_wide, scores, d_probs, probs, d_scores, att, dq, kv_grad,
    parts, far_two, far_parts, base_t,
    give, take, far_send, far_recv, near_send, near_recv, line,
    far2_recv, near2_send, near2_recv, z_part, total,
    grads, g_mate, g_half, gz_recv, g_plane, gp_recv,
    load_s, as_, ar, mate_s, mate_r, ls, lr, zs, zr,
    give_s, take_s, s1s, s1r, s2s, s2r, gs, gr,
):
    r, c, a, b = place()
    d = lax.axis_index("dev")
    x, y = lax.rem(lax.div(d, 2), 4), lax.div(d, 8)
    ak, bk, rk = around(a), around(b), around(r)
    mate = (r, d + 1 - 2 * c)
    a_to = [(r, dev_at(k, b, c)) for k in ak]
    b_to = [(r, dev_at(a, k, c)) for k in bk]
    z_to = [(k, d) for k in rk]

    def peer_at(q):
        return (r, (turn(y, lax.div(q, 4)) * 4 + turn(x, lax.rem(q, 4))) * 2 + c)

    loads = []
    for n, (src, dst) in enumerate(((wq_hbm, wq), (cot_hbm, cot), (wo_hbm, wo), (wk_hbm, wk), (wv_hbm, wv))):
        load = pltpu.make_async_copy(src, dst, load_s.at[n])
        load.start()
        loads.append(load)
    barrier = pltpu.get_barrier_semaphore()
    for peer in [mate] + z_to[1:]:
        pl.semaphore_signal(barrier, inc=1, device_id=peer, device_id_type=MESH)

    def greet(q, _):
        pl.semaphore_signal(barrier, inc=1, device_id=peer_at(q), device_id_type=MESH)
        return 0

    lax.fori_loop(1, 16, greet, 0)
    marks[...] = jnp.zeros((8, 128), jnp.int32)
    marks[:2] = labels[...]
    pl.semaphore_wait(barrier, 19)
    started = []

    def send(src, dst, s, q, to):
        copy = remote(src, dst, s, q, to)
        copy.start()
        started.append(copy)

    def got(dst, s, q):
        remote(dst, dst, s, q, mate).wait_recv()

    def gather():
        def slot(i, j):
            return g.at[c, bk[j], ak[i]]

        def run(n, src, dst, to):
            send(src, dst, as_.at[n], ar.at[n], to)

        def arrived(n, dst):
            got(dst, as_.at[n], ar.at[n])

        def cross(i, j):
            src = states if i == 0 and j == 0 else slot(i, j)
            send(src, slot(i, j), mate_s.at[i * 4 + j], mate_r.at[i * 4 + j], mate)

        run(0, states, slot(0, 0), a_to[2])
        run(1, states, slot(0, 0), a_to[1])
        run(4, states, slot(0, 0), b_to[2])
        run(5, states, slot(0, 0), b_to[1])
        row = gl.at[c, b, a]
        send(marks, row, ls.at[0], lr.at[0], a_to[2])
        send(marks, row, ls.at[1], lr.at[1], a_to[1])
        send(states, far, zs.at[0], zr.at[0], z_to[1])
        send(marks, fl, zs.at[1], zr.at[1], z_to[1])
        cross(0, 0)
        g[c, b, a] = states[...]
        gl[c, b, a] = marks[...]
        yield
        arrived(0, slot(1, 0))
        run(2, slot(1, 0).at[0], slot(1, 0).at[0], a_to[2])
        run(8, slot(1, 0), slot(1, 0), b_to[2])
        run(9, slot(1, 0), slot(1, 0), b_to[1])
        arrived(1, slot(2, 0))
        run(3, slot(2, 0).at[1], slot(2, 0).at[1], a_to[1])
        run(12, slot(2, 0), slot(2, 0), b_to[2])
        run(13, slot(2, 0), slot(2, 0), b_to[1])

        def second(i):
            n = 4 + 4 * i
            arrived(n, slot(i, 1))
            run(n + 2, slot(i, 1).at[0], slot(i, 1).at[0], b_to[2])
            arrived(n + 1, slot(i, 2))
            run(n + 3, slot(i, 2).at[1], slot(i, 2).at[1], b_to[1])
            cross(i, 1)
            cross(i, 2)

        second(0)
        cross(1, 0)
        cross(2, 0)
        got(gl.at[c, b, ak[1]], ls.at[0], lr.at[0])
        send(gl.at[c, b, ak[1]], gl.at[c, b, ak[1]], ls.at[2], lr.at[2], a_to[2])
        got(gl.at[c, b, ak[2]], ls.at[1], lr.at[1])
        yield
        arrived(2, slot(3, 0).at[0])
        arrived(3, slot(3, 0).at[1])
        run(16, slot(3, 0), slot(3, 0), b_to[2])
        run(17, slot(3, 0), slot(3, 0), b_to[1])
        cross(3, 0)
        got(gl.at[c, b, ak[3]], ls.at[2], lr.at[2])
        send(gl.at[c, b], gl.at[c, b], ls.at[3], lr.at[3], b_to[2])
        send(gl.at[c, b], gl.at[c, b], ls.at[4], lr.at[4], b_to[1])
        yield
        second(1)
        yield
        second(2)
        got(gl.at[c, bk[1]], ls.at[3], lr.at[3])
        send(gl.at[c, bk[1]], gl.at[c, bk[1]], ls.at[5], lr.at[5], b_to[2])
        got(gl.at[c, bk[2]], ls.at[4], lr.at[4])
        yield
        second(3)
        got(gl.at[c, bk[3]], ls.at[5], lr.at[5])
        send(gl.at[c], gl.at[c], ls.at[6], lr.at[6], mate)
        for i in range(4):
            n = 4 + 4 * i
            arrived(n + 2, slot(i, 3).at[0])
            arrived(n + 3, slot(i, 3).at[1])
            cross(i, 3)
        for i in range(4):
            for j in range(4):
                got(g.at[1 - c, ak[j], bk[i]], mate_s.at[i * 4 + j], mate_r.at[i * 4 + j])
        got(gl.at[1 - c], ls.at[6], lr.at[6])
        yield

    gain_row = gain[...]

    def own_rows():
        for n in range(3):
            loads[n].wait()
        for k in range(2):
            rows = slice(k * 128, (k + 1) * 128)
            normed[rows] = normalize(states[k], gain_row)
            normed_keys[k, :128] = normed[rows]
        q_own[...] = (dot(normed[...], wq[...]).astype(BF16) * 0.125).astype(BF16)
        d_att[...] = dot(cot[...], wo[...], NT).astype(BF16)

    def project(k, rows):
        n = normed_keys[k, rows]
        keys[k, rows] = dot(n, wk[...]).astype(BF16)
        values[k, rows] = dot(n, wv[...]).astype(BF16)

    def own_keys():
        for n in (3, 4):
            loads[n].wait()
        for k in range(2):
            project(k, slice(0, 128))
            key_marks[k, :, :128] = jnp.broadcast_to(marks[k : k + 1], (8, 128)).astype(F32)

    def far_keys():
        got(far, zs.at[0], zr.at[0])
        got(fl, zs.at[1], zr.at[1])
        for k in range(2):
            m = lax.rem(near_ref[k, 5], 2)
            normed_keys[k, 640:] = normalize(far[m], gain_row)
            project(k, slice(640, 768))
            key_marks[k, :, 640:] = jnp.broadcast_to(fl[pl.ds(m, 1)], (8, 128)).astype(F32)

    def plan_parts():
        wanted = [lax.rem(near_ref[k, 1 + e], 64) for k in range(2) for e in range(4)]

        def look(t, _):
            found = jnp.int32(8)
            for n, block in enumerate(wanted):
                found = jnp.where(block == t, n, found)
            table[t] = found
            return 0

        lax.fori_loop(0, 64, look, 0)
        parts[8] = jnp.zeros((512, 128), BF16)

    def fetch(k, e):
        block = near_ref[k, 1 + e]
        at = lax.rem(lax.div(block, 2), 32)
        core = lax.rem(at, 2)
        ax = lax.rem(lax.div(at, 2), 4)
        ay = lax.div(at, 8)
        first, second = ax * (1 - core) + ay * core, ay * (1 - core) + ax * core
        local = lax.rem(block, 2)
        rows = slice((1 + e) * 128, (2 + e) * 128)
        normed_keys[k, rows] = normalize(g[core, second, first, local], gain_row)
        key_marks[k, :, rows] = jnp.broadcast_to(gl[core, second, first, pl.ds(local, 1)], (8, 128)).astype(F32)

    def fetched_keys():
        for k in range(2):
            for e in range(4):
                fetch(k, e)
        for k in range(2):
            def one(e, _, k=k):
                project(k, span(128 + e * 256, 256))
                return 0

            lax.fori_loop(0, 2, one, 0)
        for k in range(2):
            own = jnp.broadcast_to(marks[k : k + 1], (128, 128)).astype(F32).T
            for e in range(6):
                at = slice(e * 128, (e + 1) * 128)
                gap = jnp.abs(own - jnp.broadcast_to(key_marks[k, :1, at], (128, 128)))
                bias[k, :, at] = jnp.where(gap <= 1.0, 0.0, -jnp.inf)

    head_of = lax.broadcasted_iota(jnp.int32, (128, 256), 1) // 64

    def attend(n, _):
        k, half = lax.div(n, 2), lax.rem(n, 2)
        rows = pl.ds(pl.multiple_of(k * 128, 128), 128)
        cols = pl.ds(pl.multiple_of(half * 256, 256), 256)
        for i in range(4):
            at = slice(i * 128, (i + 1) * 128)
            q_wide[at] = jnp.where(head_of == i, q_own[rows, cols].astype(F32), 0.0).astype(BF16)
            d_wide[at] = jnp.where(head_of == i, d_att[rows, cols].astype(F32), 0.0).astype(BF16)
        scores[...] = dot(q_wide[...], keys[k, :, cols], NT)
        d_probs[...] = dot(d_wide[...], values[k, :, cols], NT)

        def soft(t, _):
            at = pl.ds(pl.multiple_of(t * 128, 128), 128)
            w = jnp.exp(scores[at] + bias[k])
            p = w * (1.0 / jnp.sum(w, axis=-1, keepdims=True))
            dp = d_probs[at]
            mean = jnp.sum(p * dp, axis=-1, keepdims=True)
            probs[at] = p.astype(BF16)
            d_scores[at] = (p * (dp - mean)).astype(BF16)
            return 0

        lax.fori_loop(0, 4, soft, 0, unroll=2)
        mixed = dot(probs[...], values[k, :, cols])
        turned = dot(d_scores[...], keys[k, :, cols])
        one = jnp.zeros((128, 256), F32)
        two = jnp.zeros((128, 256), F32)
        for i in range(4):
            at = slice(i * 128, (i + 1) * 128)
            one = one + jnp.where(head_of == i, mixed[at], 0.0)
            two = two + jnp.where(head_of == i, turned[at], 0.0)
        att[rows, cols] = one.astype(BF16)
        dq[rows, cols] = (two * 0.125).astype(BF16)
        kv_grad[k, cols] = dot(q_wide[...], d_scores[...], TN).astype(BF16)
        kv_grad[k, pl.ds(pl.multiple_of(512 + half * 256, 256), 256)] = dot(d_wide[...], probs[...], TN).astype(BF16)
        return 0

    def hold(p, m, value):
        for half in range(2):
            grads[p, pl.ds(m * 1024 + half * 512, 512)] = value[:, half * 256 : (half + 1) * 256].astype(BF16)

    def query_output():
        hold(0, 0, dot(normed[...], dq[...], TN))
        hold(0, 1, dot(att[...], cot[...], TN))

    def key_value():
        for m in range(2):
            at = slice(m * 512, (m + 1) * 512)
            hold(1, m, (dot(kv_grad[0, at], normed_keys[0]) + dot(kv_grad[1, at], normed_keys[1])).T)

    def part_of(k, at):
        return dot(wk[...], kv_grad[k, :512, at]) + dot(wv[...], kv_grad[k, 512:, at])

    def near_parts(k):
        for pair in range(2):
            value = part_of(k, slice(128 + pair * 256, 384 + pair * 256)).astype(BF16)
            for e in range(2):
                parts[k * 4 + pair * 2 + e] = value[:, e * 128 : (e + 1) * 128]

    def edge_parts():
        for k in range(2):
            far_two[k] = part_of(k, slice(640, 768)).astype(BF16)
        m = lax.rem(near_ref[0, 5], 2)
        for k in range(2):
            far_parts[k] = far_two[lax.rem(k + m, 2)]
        send(far_parts, z_part, zs.at[2], zr.at[2], z_to[2])

    def own_parts():
        mine = dot(wq[...], dq[...], NT)
        for k in range(2):
            at = slice(k * 128, (k + 1) * 128)
            base_t[:, at] = mine[:, at] + part_of(k, slice(0, 128)).astype(BF16).astype(F32)
        branch[...] = dot(att[...], wo[...]).astype(BF16)

    def each(work):
        def step(t, _):
            work(pl.ds(pl.multiple_of(t * 128, 128), 128))
            return 0

        lax.fori_loop(0, 4, step, 0)

    def here(i, j, block, rows):
        mine = parts[table[2 * dev_at(ak[i], bk[j], c) + block], rows]
        return mine.astype(F32) + take[i * 4 + j, block, rows].astype(F32)

    def took(i, j):
        got(take.at[i * 4 + j], give_s.at[i * 4 + j], take_s.at[i * 4 + j])

    order = (3, 1, 2, 0)

    def exchange(j):
        for i in order:
            n = i * 4 + j
            for block in range(2):
                give[n, block] = parts[table[2 * dev_at(bk[i], ak[j], 1 - c) + block]]
            send(give.at[n], take.at[n], give_s.at[n], take_s.at[n], mate)

    def rings():
        for i in order:
            took(i, 3)
            for block in range(2):
                def far_sum(rows, block=block, i=i):
                    far_send[i, block, rows] = here(i, 3, block, rows).astype(BF16)

                each(far_sum)
                send(far_send.at[i, block], far_recv.at[i, block], s1s.at[i * 4 + block], s1r.at[i * 4 + block], b_to[2 - block])
        yield
        for i in order:
            for way in range(2):
                j = 2 - way
                took(i, j)
                got(far_recv.at[i, way], s1s.at[i * 4 + way], s1r.at[i * 4 + way])

                def near_sum(rows, way=way, i=i, j=j):
                    near_send[i, way, way, rows] = (here(i, j, way, rows) + far_recv[i, way, rows].astype(F32)).astype(BF16)
                    near_send[i, way, 1 - way, rows] = here(i, j, 1 - way, rows).astype(BF16)

                each(near_sum)
                send(near_send.at[i, way], near_recv.at[i, way], s1s.at[i * 4 + 2 + way], s1r.at[i * 4 + 2 + way], b_to[j])
            yield

        def ring_end(i):
            took(i, 0)
            for way in range(2):
                got(near_recv.at[i, way], s1s.at[i * 4 + 2 + way], s1r.at[i * 4 + 2 + way])
            for block in range(2):
                def end(rows, block=block):
                    line[i, block, rows] = (
                        here(i, 0, block, rows) + near_recv[i, 0, block, rows].astype(F32)
                        + near_recv[i, 1, block, rows].astype(F32)).astype(BF16)

                each(end)

        ring_end(3)
        for block in range(2):
            send(line.at[3, block], far2_recv.at[block], s2s.at[block], s2r.at[block], a_to[2 - block])
        yield
        for way in (1, 0):
            ring_end(2 - way)
            got(far2_recv.at[way], s2s.at[way], s2r.at[way])

            def near2(rows, way=way):
                near2_send[way, way, rows] = (line[2 - way, way, rows].astype(F32) + far2_recv[way, rows].astype(F32)).astype(BF16)
                near2_send[way, 1 - way, rows] = line[2 - way, 1 - way, rows]

            each(near2)
            send(near2_send.at[way], near2_recv.at[way], s2s.at[2 + way], s2r.at[2 + way], a_to[2 - way])
            yield
        ring_end(0)
        yield
        for way in range(2):
            got(near2_recv.at[way], s2s.at[2 + way], s2r.at[2 + way])
        got(z_part, zs.at[2], zr.at[2])
        for block in range(2):
            def last(rows, block=block):
                at = slice(block * 128, block * 128 + 128)
                total[rows, at] = (
                    base_t[rows, at] + line[0, block, rows].astype(F32) + near2_recv[0, block, rows].astype(F32)
                    + near2_recv[1, block, rows].astype(F32) + z_part[block, rows].astype(F32))

            each(last)
        for block in range(2):
            rows = slice(block * 128, block * 128 + 128)
            d_normed = total[:, rows].T
            wide = states[block].astype(F32)
            inverse = lax.rsqrt(jnp.mean(wide * wide, axis=-1, keepdims=True) + EPSILON)
            scaled = d_normed * gain_row
            along = jnp.sum(scaled * wide, axis=-1, keepdims=True) * (1.0 / 512)
            grad_states[rows] = (inverse * scaled - wide * (inverse * inverse * inverse * along)).astype(BF16)
        yield

    base = c * 1024

    def chunk_at(q):
        return (turn(y, lax.div(q, 4)) * 4 + turn(x, lax.rem(q, 4))) * 16

    def other_way(q):
        return lax.rem(4 - lax.div(q, 4), 4) * 4 + lax.rem(4 - lax.rem(q, 4), 4)

    def weights(p):
        at = p * 38
        whole = summed.at[p]
        send(grads.at[p, span(1024 - base, 1024)], g_mate.at[p], gs.at[at], gr.at[at], mate)
        yield
        got(g_mate.at[p], gs.at[at], gr.at[at])

        def half_sum(t, _):
            rows = span(t * 128, 128)
            g_half[p, rows] = (grads[p, span(base + t * 128, 128)].astype(F32) + g_mate[p, rows].astype(F32)).astype(BF16)
            return 0

        lax.fori_loop(0, 8, half_sum, 0)
        for k in range(1, 4):
            send(g_half.at[p, span(rk[k] * 256, 256)], gz_recv.at[p, k - 1], gs.at[at + k], gr.at[at + k], z_to[k])
        yield
        for k in range(1, 4):
            got(gz_recv.at[p, k - 1], gs.at[at + k], gr.at[at + k])

        def z_sum(t, _):
            rows = span(t * 64, 64)
            g_plane[p, rows] = (
                g_half[p, span(r * 256 + t * 64, 64)].astype(F32) + gz_recv[p, 0, rows].astype(F32)
                + gz_recv[p, 1, rows].astype(F32) + gz_recv[p, 2, rows].astype(F32)).astype(BF16)
            return 0

        lax.fori_loop(0, 4, z_sum, 0)

        def plane_out(q):
            return remote(
                g_plane.at[p, span(chunk_at(q), 16)], gp_recv.at[p, q - 1],
                gs.at[at + 3 + q], gr.at[at + 3 + q], peer_at(q))

        def begin(q, _):
            plane_out(q).start()
            return 0

        lax.fori_loop(1, 16, begin, 0)
        yield

        def plane_sum(q, held):
            plane_out(q).wait()
            return held + gp_recv[p, q - 1].astype(F32)

        held = lax.fori_loop(1, 16, plane_sum, g_plane[p, span(chunk_at(0), 16)].astype(F32))
        mine = span(base + r * 256 + chunk_at(0), 16)
        summed[p, mine] = held.astype(BF16)

        def back_out(q):
            return remote(whole.at[mine], whole.at[mine], gs.at[at + 18 + q], gr.at[at + 18 + q], peer_at(q))

        def begin_back(q, _):
            back_out(q).start()
            return 0

        lax.fori_loop(1, 16, begin_back, 0)
        yield

        def end_back(q, _):
            back_out(q).wait_send()
            there = whole.at[span(base + r * 256 + chunk_at(other_way(q)), 16)]
            remote(there, there, gs.at[at + 18 + q], gr.at[at + 18 + q], mate).wait_recv()
            return 0

        lax.fori_loop(1, 16, end_back, 0)
        line_part = whole.at[span(base + r * 256, 256)]
        for k in range(1, 4):
            send(line_part, line_part, gs.at[at + 33 + k], gr.at[at + 33 + k], z_to[k])
        yield
        for k, source in ((1, rk[2]), (2, rk[1]), (3, rk[3])):
            got(whole.at[span(base + source * 256, 256)], gs.at[at + 33 + k], gr.at[at + 33 + k])
        half = whole.at[span(base, 1024)]
        send(half, half, gs.at[at + 37], gr.at[at + 37], mate)
        yield
        got(whole.at[span(1024 - base, 1024)], gs.at[at + 37], gr.at[at + 37])
        yield

    states_in, first, second, ring = gather(), weights(0), weights(1), rings()
    next(states_in)
    own_rows()
    own_keys()
    plan_parts()
    next(states_in)
    far_keys()
    for _ in range(4):
        next(states_in)
    fetched_keys()
    lax.fori_loop(0, 4, attend, 0)
    query_output()
    next(first)
    near_parts(0)
    near_parts(1)
    next(first)
    for j in (3, 1, 2, 0):
        exchange(j)
    key_value()
    next(second)
    next(ring)
    next(first)
    edge_parts()
    next(second)
    next(ring)
    next(first)
    own_parts()
    for step in PLAN:
        next({"w": first, "v": second, "r": ring}[step])
    for copy in started:
        copy.wait_send()


PLAN = "rrwvrrwvrrwrrvvv"


def layer(neighbours, states, gain, labels, wq, wk, wv, wo, cot):
    vmem = pl.BlockSpec(memory_space=pltpu.VMEM)
    smem = pl.BlockSpec(memory_space=pltpu.SMEM)
    anywhere = pl.BlockSpec(memory_space=pl.ANY)
    dma = pltpu.SemaphoreType.DMA

    def half(*shape):
        return pltpu.VMEM(shape, BF16)

    def full(*shape):
        return pltpu.VMEM(shape, F32)

    def whole(*shape):
        return pltpu.VMEM(shape, jnp.int32)

    return pl.pallas_call(
        layer_kernel,
        out_shape=(
            jax.ShapeDtypeStruct((256, 512), BF16),
            jax.ShapeDtypeStruct((256, 512), BF16),
            jax.ShapeDtypeStruct((2, 2048, 256), BF16),
        ),
        in_specs=[smem] + [vmem] * 3 + [anywhere] * 5,
        out_specs=[vmem] * 3,
        scratch_shapes=[
            half(512, 512), half(512, 512), half(512, 512), half(512, 512), half(256, 512),
            whole(8, 128), half(2, 4, 4, 2, 128, 512), whole(2, 4, 4, 8, 128), half(2, 128, 512), whole(8, 128),
            pltpu.SMEM((64,), jnp.int32),
            half(256, 512), half(256, 512), half(256, 512),
            half(2, 768, 512), half(2, 768, 512), half(2, 768, 512), full(2, 8, 768), full(2, 128, 768),
            half(512, 256), half(512, 256), full(512, 768), full(512, 768), half(512, 768), half(512, 768),
            half(256, 512), half(256, 512), half(2, 1024, 768),
            half(9, 512, 128), half(2, 512, 128), half(2, 512, 128), full(512, 256),
            half(16, 2, 512, 128), half(16, 2, 512, 128),
            half(4, 2, 512, 128), half(4, 2, 512, 128),
            half(4, 2, 2, 512, 128), half(4, 2, 2, 512, 128), half(4, 2, 512, 128),
            half(2, 512, 128), half(2, 2, 512, 128), half(2, 2, 512, 128), half(2, 512, 128), full(512, 256),
            half(2, 2048, 256), half(2, 1024, 256), half(2, 1024, 256), half(2, 3, 256, 256),
            half(2, 256, 256), half(2, 15, 16, 256),
            dma((5,)), dma((20,)), dma((20,)), dma((16,)), dma((16,)), dma((7,)), dma((7,)), dma((3,)), dma((3,)),
            dma((16,)), dma((16,)), dma((16,)), dma((16,)), dma((4,)), dma((4,)), dma((76,)), dma((76,)),
        ],
        compiler_params=pltpu.CompilerParams(collective_id=0, has_side_effects=True, vmem_limit_bytes=VMEM_LIMIT),
    )(neighbours, states, gain, labels, wq, wk, wv, wo, cot)


def body(states, norm_gain, w_query, w_key, w_value, w_out, neighbours, labels, cotangent):
    branch_out, grad_states, summed = layer(
        neighbours, states.reshape(2, 128, 512), norm_gain.reshape(1, -1), labels, w_query, w_key, w_value, w_out, cotangent)
    scale = 1.0 / math.sqrt(32768)
    split = summed.reshape(2, 2, 2, 512, 256)

    def joined(p, m):
        return jnp.concatenate([split[p, m, 0], split[p, m, 1]], axis=1).astype(F32) * scale

    grad_query, grad_output, grad_key, grad_value = joined(0, 0), joined(0, 1), joined(1, 0), joined(1, 1)
    along = grad_query * w_query.astype(F32) + grad_key * w_key.astype(F32) + grad_value * w_value.astype(F32)
    grad_gain = jnp.sum(along, axis=1) / norm_gain
    return branch_out, grad_states, grad_query, grad_key, grad_value, grad_output, grad_gain


def solution(mesh):
    rows = P(("region", "dev"), None)
    return jax.shard_map(
        body, mesh=mesh,
        in_specs=(rows, P(), P(), P(), P(), P(), rows, rows, rows),
        out_specs=(rows, rows, P(), P(), P(), P(), P()),
        check_vma=False)
```

```python
import math

import jax
import jax.numpy as jnp
from jax import lax
from jax.experimental import pallas as pl
from jax.experimental.pallas import tpu as pltpu
from jax.sharding import PartitionSpec as P

MESH = pl.DeviceIdType.MESH
HEADS = 8
EPSILON = 1e-05
F32 = jnp.float32
BF16 = jnp.bfloat16
VMEM_LIMIT = 56 * 1024 * 1024
NN = (((1,), (0,)), ((), ()))
NT = (((1,), (1,)), ((), ()))
TN = (((0,), (0,)), ((), ()))


def dot(left, right, how=NN):
    return lax.dot_general(left, right, how, preferred_element_type=F32)


def place():
    r = lax.axis_index("region")
    d = lax.axis_index("dev")
    c = lax.rem(d, 2)
    x = lax.rem(lax.div(d, 2), 4)
    y = lax.div(d, 8)
    return r, c, x * (1 - c) + y * c, y * (1 - c) + x * c


def turn(value, step):
    return lax.rem(value + step + 4, 4)


def dev_at(a, b, c):
    return ((b * (1 - c) + a * c) * 4 + a * (1 - c) + b * c) * 2 + c


def around(value):
    return [value, turn(value, -1), turn(value, 1), turn(value, 2)]


def normalize(rows, gain):
    wide = rows.astype(F32)
    inverse = lax.rsqrt(jnp.mean(wide * wide, axis=-1, keepdims=True) + EPSILON)
    return (wide * inverse * gain).astype(BF16)


def remote(src, dst, s, q, to):
    return pltpu.make_async_remote_copy(
        src_ref=src, dst_ref=dst, send_sem=s, recv_sem=q, device_id=to, device_id_type=MESH)


def span(first, size):
    return pl.ds(pl.multiple_of(first, 16), size)


def layer_kernel(
    near_ref, states, gain, labels, wq_hbm, wk_hbm, wv_hbm, wo_hbm, cot_hbm,
    branch, grad_states, summed,
    wq, wk, wv, wo, cot, marks, g, gl, far, fl, table,
    normed, q_own, d_att, keys, normed_keys, values, key_marks, bias,
    q_wide, d_wide, scores, d_probs, probs, d_scores, att, dq, kv_grad,
    parts, far_two, far_parts, base_t,
    give, take, far_send, far_recv, near_send, near_recv, line,
    far2_recv, near2_send, near2_recv, z_part, total,
    grads, g_mate, g_half, gz_recv, g_plane, gp_recv,
    load_s, as_, ar, mate_s, mate_r, ls, lr, zs, zr,
    give_s, take_s, s1s, s1r, s2s, s2r, gs, gr,
):
    r, c, a, b = place()
    d = lax.axis_index("dev")
    x, y = lax.rem(lax.div(d, 2), 4), lax.div(d, 8)
    ak, bk, rk = around(a), around(b), around(r)
    mate = (r, d + 1 - 2 * c)
    a_to = [(r, dev_at(k, b, c)) for k in ak]
    b_to = [(r, dev_at(a, k, c)) for k in bk]
    z_to = [(k, d) for k in rk]

    def peer_at(q):
        return (r, (turn(y, lax.div(q, 4)) * 4 + turn(x, lax.rem(q, 4))) * 2 + c)

    loads = []
    for n, (src, dst) in enumerate(((wq_hbm, wq), (cot_hbm, cot), (wo_hbm, wo), (wk_hbm, wk), (wv_hbm, wv))):
        load = pltpu.make_async_copy(src, dst, load_s.at[n])
        load.start()
        loads.append(load)
    barrier = pltpu.get_barrier_semaphore()
    for peer in [mate] + z_to[1:]:
        pl.semaphore_signal(barrier, inc=1, device_id=peer, device_id_type=MESH)

    def greet(q, _):
        pl.semaphore_signal(barrier, inc=1, device_id=peer_at(q), device_id_type=MESH)
        return 0

    lax.fori_loop(1, 16, greet, 0)
    marks[...] = jnp.zeros((8, 128), jnp.int32)
    marks[:2] = labels[...]
    pl.semaphore_wait(barrier, 19)
    started = []

    def send(src, dst, s, q, to):
        copy = remote(src, dst, s, q, to)
        copy.start()
        started.append(copy)

    def got(dst, s, q):
        remote(dst, dst, s, q, mate).wait_recv()

    def gather():
        def slot(i, j):
            return g.at[c, bk[j], ak[i]]

        def first_in(n, i, half):
            got(slot(i, 0).at[half], as_.at[n], ar.at[n])

        def out(n, src, dst, to):
            send(src, dst, as_.at[n], ar.at[n], to)

        def cross(i, j):
            src = states if i == 0 and j == 0 else slot(i, j)
            send(src, slot(i, j), mate_s.at[i * 4 + j], mate_r.at[i * 4 + j], mate)

        def second_out(i, half, way):
            src = states if i == 0 else slot(i, 0)
            out(6 + 6 * i + 2 * way + half, src.at[half], slot(i, 0).at[half], b_to[2 - way])

        def second_in(i, half, way):
            n = 6 + 6 * i + 2 * way + half
            got(slot(i, 1 + way).at[half], as_.at[n], ar.at[n])

        def second_on(i, way):
            second_in(i, way, way)
            there = slot(i, 1 + way).at[way]
            out(10 + 6 * i + way, there, there, b_to[2 - way])

        def first_on(way):
            first_in(2 * way + way, 1 + way, way)
            there = slot(1 + way, 0).at[way]
            out(4 + way, there, there, a_to[2 - way])

        for block in range(2):
            for way in range(2):
                half = block if way == 0 else 1 - block
                out(2 * way + half, states.at[half], slot(0, 0).at[half], a_to[2 - way])
            for way in range(2):
                second_out(0, block if way == 0 else 1 - block, way)
        row = gl.at[c, b, a]
        send(marks, row, ls.at[0], lr.at[0], a_to[2])
        send(marks, row, ls.at[1], lr.at[1], a_to[1])
        send(states, far, zs.at[0], zr.at[0], z_to[1])
        send(marks, fl, zs.at[1], zr.at[1], z_to[1])
        cross(0, 0)
        g[c, b, a] = states[...]
        gl[c, b, a] = marks[...]
        yield
        for way in range(2):
            first_on(way)
            second_out(1 + way, way, way)
            second_out(1 + way, way, 1 - way)
        for way in range(2):
            second_on(0, way)
        for way in range(2):
            first_in(2 * way + 1 - way, 1 + way, 1 - way)
            second_out(1 + way, 1 - way, 1 - way)
            second_out(1 + way, 1 - way, way)
            cross(1 + way, 0)
        for way in range(2):
            second_in(0, 1 - way, way)
            cross(0, 1 + way)
        got(gl.at[c, b, ak[1]], ls.at[0], lr.at[0])
        send(gl.at[c, b, ak[1]], gl.at[c, b, ak[1]], ls.at[2], lr.at[2], a_to[2])
        got(gl.at[c, b, ak[2]], ls.at[1], lr.at[1])
        yield
        for way in range(2):
            got(slot(3, 0).at[way], as_.at[4 + way], ar.at[4 + way])
            second_out(3, way, way)
            second_out(3, way, 1 - way)
        cross(3, 0)
        got(gl.at[c, b, ak[3]], ls.at[2], lr.at[2])
        send(gl.at[c, b], gl.at[c, b], ls.at[3], lr.at[3], b_to[2])
        send(gl.at[c, b], gl.at[c, b], ls.at[4], lr.at[4], b_to[1])
        yield
        for way in range(2):
            second_on(1 + way, way)
        for way in range(2):
            second_on(2 - way, way)
        for i in (1, 2):
            for way in range(2):
                second_in(i, 1 - way, way)
                cross(i, 1 + way)
        yield
        got(gl.at[c, bk[1]], ls.at[3], lr.at[3])
        send(gl.at[c, bk[1]], gl.at[c, bk[1]], ls.at[5], lr.at[5], b_to[2])
        got(gl.at[c, bk[2]], ls.at[4], lr.at[4])
        for way in range(2):
            second_on(3, way)
        for way in range(2):
            second_in(3, 1 - way, way)
            cross(3, 1 + way)
        yield
        got(gl.at[c, bk[3]], ls.at[5], lr.at[5])
        send(gl.at[c], gl.at[c], ls.at[6], lr.at[6], mate)
        for i in range(4):
            for way in range(2):
                got(slot(i, 3).at[way], as_.at[10 + 6 * i + way], ar.at[10 + 6 * i + way])
            cross(i, 3)
        for i in range(4):
            for j in range(4):
                got(g.at[1 - c, ak[j], bk[i]], mate_s.at[i * 4 + j], mate_r.at[i * 4 + j])
        got(gl.at[1 - c], ls.at[6], lr.at[6])
        yield

    gain_row = gain[...]

    def own_rows():
        for n in range(3):
            loads[n].wait()
        for k in range(2):
            rows = slice(k * 128, (k + 1) * 128)
            normed[rows] = normalize(states[k], gain_row)
            normed_keys[k, :128] = normed[rows]
        q_own[...] = (dot(normed[...], wq[...]).astype(BF16) * 0.125).astype(BF16)
        d_att[...] = dot(cot[...], wo[...], NT).astype(BF16)

    def project(k, rows):
        n = normed_keys[k, rows]
        keys[k, rows] = dot(n, wk[...]).astype(BF16)
        values[k, rows] = dot(n, wv[...]).astype(BF16)

    def own_keys():
        for n in (3, 4):
            loads[n].wait()
        for k in range(2):
            project(k, slice(0, 128))
            key_marks[k, :, :128] = jnp.broadcast_to(marks[k : k + 1], (8, 128)).astype(F32)

    def far_keys():
        got(far, zs.at[0], zr.at[0])
        got(fl, zs.at[1], zr.at[1])
        for k in range(2):
            m = lax.rem(near_ref[k, 5], 2)
            normed_keys[k, 640:] = normalize(far[m], gain_row)
            project(k, slice(640, 768))
            key_marks[k, :, 640:] = jnp.broadcast_to(fl[pl.ds(m, 1)], (8, 128)).astype(F32)

    def plan_parts():
        wanted = [lax.rem(near_ref[k, 1 + e], 64) for k in range(2) for e in range(4)]

        def look(t, _):
            found = jnp.int32(8)
            for n, block in enumerate(wanted):
                found = jnp.where(block == t, n, found)
            table[t] = found
            return 0

        lax.fori_loop(0, 64, look, 0)
        parts[8] = jnp.zeros((512, 128), BF16)

    def fetch(k, e):
        block = near_ref[k, 1 + e]
        at = lax.rem(lax.div(block, 2), 32)
        core = lax.rem(at, 2)
        ax = lax.rem(lax.div(at, 2), 4)
        ay = lax.div(at, 8)
        first, second = ax * (1 - core) + ay * core, ay * (1 - core) + ax * core
        local = lax.rem(block, 2)
        rows = slice((1 + e) * 128, (2 + e) * 128)
        normed_keys[k, rows] = normalize(g[core, second, first, local], gain_row)
        key_marks[k, :, rows] = jnp.broadcast_to(gl[core, second, first, pl.ds(local, 1)], (8, 128)).astype(F32)

    def fetched_keys():
        for k in range(2):
            for e in range(4):
                fetch(k, e)
        for k in range(2):
            def one(e, _, k=k):
                project(k, span(128 + e * 256, 256))
                return 0

            lax.fori_loop(0, 2, one, 0)
        for k in range(2):
            own = jnp.broadcast_to(marks[k : k + 1], (128, 128)).astype(F32).T
            for e in range(6):
                at = slice(e * 128, (e + 1) * 128)
                gap = jnp.abs(own - jnp.broadcast_to(key_marks[k, :1, at], (128, 128)))
                bias[k, :, at] = jnp.where(gap <= 1.0, 0.0, -jnp.inf)

    head_of = lax.broadcasted_iota(jnp.int32, (128, 256), 1) // 64

    def attend(n, _):
        k, half = lax.div(n, 2), lax.rem(n, 2)
        rows = pl.ds(pl.multiple_of(k * 128, 128), 128)
        cols = pl.ds(pl.multiple_of(half * 256, 256), 256)
        for i in range(4):
            at = slice(i * 128, (i + 1) * 128)
            q_wide[at] = jnp.where(head_of == i, q_own[rows, cols].astype(F32), 0.0).astype(BF16)
            d_wide[at] = jnp.where(head_of == i, d_att[rows, cols].astype(F32), 0.0).astype(BF16)
        scores[...] = dot(q_wide[...], keys[k, :, cols], NT)
        d_probs[...] = dot(d_wide[...], values[k, :, cols], NT)

        def soft(t, _):
            at = pl.ds(pl.multiple_of(t * 128, 128), 128)
            w = jnp.exp(scores[at] + bias[k])
            p = w * (1.0 / jnp.sum(w, axis=-1, keepdims=True))
            dp = d_probs[at]
            mean = jnp.sum(p * dp, axis=-1, keepdims=True)
            probs[at] = p.astype(BF16)
            d_scores[at] = (p * (dp - mean)).astype(BF16)
            return 0

        lax.fori_loop(0, 4, soft, 0, unroll=2)
        mixed = dot(probs[...], values[k, :, cols])
        turned = dot(d_scores[...], keys[k, :, cols])
        one = jnp.zeros((128, 256), F32)
        two = jnp.zeros((128, 256), F32)
        for i in range(4):
            at = slice(i * 128, (i + 1) * 128)
            one = one + jnp.where(head_of == i, mixed[at], 0.0)
            two = two + jnp.where(head_of == i, turned[at], 0.0)
        att[rows, cols] = one.astype(BF16)
        dq[rows, cols] = (two * 0.125).astype(BF16)
        kv_grad[k, cols] = dot(q_wide[...], d_scores[...], TN).astype(BF16)
        kv_grad[k, pl.ds(pl.multiple_of(512 + half * 256, 256), 256)] = dot(d_wide[...], probs[...], TN).astype(BF16)
        return 0

    def hold(p, m, value):
        for half in range(2):
            grads[p, pl.ds(m * 1024 + half * 512, 512)] = value[:, half * 256 : (half + 1) * 256].astype(BF16)

    def query_output():
        hold(0, 0, dot(normed[...], dq[...], TN))
        hold(0, 1, dot(att[...], cot[...], TN))

    def key_value():
        for m in range(2):
            at = slice(m * 512, (m + 1) * 512)
            hold(1, m, (dot(kv_grad[0, at], normed_keys[0]) + dot(kv_grad[1, at], normed_keys[1])).T)

    def part_of(k, at):
        return dot(wk[...], kv_grad[k, :512, at]) + dot(wv[...], kv_grad[k, 512:, at])

    def near_parts(k):
        for pair in range(2):
            value = part_of(k, slice(128 + pair * 256, 384 + pair * 256)).astype(BF16)
            for e in range(2):
                parts[k * 4 + pair * 2 + e] = value[:, e * 128 : (e + 1) * 128]

    def edge_parts():
        for k in range(2):
            far_two[k] = part_of(k, slice(640, 768)).astype(BF16)
        m = lax.rem(near_ref[0, 5], 2)
        for k in range(2):
            far_parts[k] = far_two[lax.rem(k + m, 2)]
        send(far_parts, z_part, zs.at[2], zr.at[2], z_to[2])

    def own_parts():
        mine = dot(wq[...], dq[...], NT)
        for k in range(2):
            at = slice(k * 128, (k + 1) * 128)
            base_t[:, at] = mine[:, at] + part_of(k, slice(0, 128)).astype(BF16).astype(F32)
        branch[...] = dot(att[...], wo[...]).astype(BF16)

    def each(work):
        def step(t, _):
            work(pl.ds(pl.multiple_of(t * 128, 128), 128))
            return 0

        lax.fori_loop(0, 4, step, 0)

    def here(i, j, block, rows):
        mine = parts[table[2 * dev_at(ak[i], bk[j], c) + block], rows]
        return mine.astype(F32) + take[i * 4 + j, block, rows].astype(F32)

    def took(i, j):
        got(take.at[i * 4 + j], give_s.at[i * 4 + j], take_s.at[i * 4 + j])

    order = (3, 1, 2, 0)

    def exchange(j):
        for i in order:
            n = i * 4 + j
            for block in range(2):
                give[n, block] = parts[table[2 * dev_at(bk[i], ak[j], 1 - c) + block]]
            send(give.at[n], take.at[n], give_s.at[n], take_s.at[n], mate)

    def rings():
        for i in order:
            took(i, 3)
            for block in range(2):
                def far_sum(rows, block=block, i=i):
                    far_send[i, block, rows] = here(i, 3, block, rows).astype(BF16)

                each(far_sum)
                send(far_send.at[i, block], far_recv.at[i, block], s1s.at[i * 4 + block], s1r.at[i * 4 + block], b_to[2 - block])
        yield
        near_copies = []
        for i in order:
            for way in range(2):
                j = 2 - way
                took(i, j)
                got(far_recv.at[i, way], s1s.at[i * 4 + way], s1r.at[i * 4 + way])

                def near_sum(rows, way=way, i=i, j=j):
                    near_send[i, way, way, rows] = (here(i, j, way, rows) + far_recv[i, way, rows].astype(F32)).astype(BF16)
                    near_send[i, way, 1 - way, rows] = here(i, j, 1 - way, rows).astype(BF16)

                each(near_sum)
                if len(near_copies) >= 2 * AHEAD:
                    near_copies[-2 * AHEAD].wait_send()
                copy = remote(near_send.at[i, way], near_recv.at[i, way], s1s.at[i * 4 + 2 + way], s1r.at[i * 4 + 2 + way], b_to[j])
                copy.start()
                near_copies.append(copy)
            yield
        started.extend(near_copies[-2 * AHEAD :])

        def ring_end(i):
            took(i, 0)
            for way in range(2):
                got(near_recv.at[i, way], s1s.at[i * 4 + 2 + way], s1r.at[i * 4 + 2 + way])
            for block in range(2):
                def end(rows, block=block):
                    line[i, block, rows] = (
                        here(i, 0, block, rows) + near_recv[i, 0, block, rows].astype(F32)
                        + near_recv[i, 1, block, rows].astype(F32)).astype(BF16)

                each(end)

        ring_end(3)
        for block in range(2):
            send(line.at[3, block], far2_recv.at[block], s2s.at[block], s2r.at[block], a_to[2 - block])
        yield
        for way in (1, 0):
            ring_end(2 - way)
            got(far2_recv.at[way], s2s.at[way], s2r.at[way])

            def near2(rows, way=way):
                near2_send[way, way, rows] = (line[2 - way, way, rows].astype(F32) + far2_recv[way, rows].astype(F32)).astype(BF16)
                near2_send[way, 1 - way, rows] = line[2 - way, 1 - way, rows]

            each(near2)
            send(near2_send.at[way], near2_recv.at[way], s2s.at[2 + way], s2r.at[2 + way], a_to[2 - way])
            yield
        ring_end(0)
        yield
        for way in range(2):
            got(near2_recv.at[way], s2s.at[2 + way], s2r.at[2 + way])
        got(z_part, zs.at[2], zr.at[2])
        for block in range(2):
            def last(rows, block=block):
                at = slice(block * 128, block * 128 + 128)
                total[rows, at] = (
                    base_t[rows, at] + line[0, block, rows].astype(F32) + near2_recv[0, block, rows].astype(F32)
                    + near2_recv[1, block, rows].astype(F32) + z_part[block, rows].astype(F32))

            each(last)
        for block in range(2):
            rows = slice(block * 128, block * 128 + 128)
            d_normed = total[:, rows].T
            wide = states[block].astype(F32)
            inverse = lax.rsqrt(jnp.mean(wide * wide, axis=-1, keepdims=True) + EPSILON)
            scaled = d_normed * gain_row
            along = jnp.sum(scaled * wide, axis=-1, keepdims=True) * (1.0 / 512)
            grad_states[rows] = (inverse * scaled - wide * (inverse * inverse * inverse * along)).astype(BF16)
        yield

    base = c * 1024

    def chunk_at(q):
        return (turn(y, lax.div(q, 4)) * 4 + turn(x, lax.rem(q, 4))) * 16

    def other_way(q):
        return lax.rem(4 - lax.div(q, 4), 4) * 4 + lax.rem(4 - lax.rem(q, 4), 4)

    def weights(p):
        at = p * 38
        whole = summed.at[p]
        send(grads.at[p, span(1024 - base, 1024)], g_mate.at[p], gs.at[at], gr.at[at], mate)
        yield
        got(g_mate.at[p], gs.at[at], gr.at[at])

        def half_sum(t, _):
            rows = span(t * 128, 128)
            g_half[p, rows] = (grads[p, span(base + t * 128, 128)].astype(F32) + g_mate[p, rows].astype(F32)).astype(BF16)
            return 0

        lax.fori_loop(0, 8, half_sum, 0)
        for k in range(1, 4):
            send(g_half.at[p, span(rk[k] * 256, 256)], gz_recv.at[p, k - 1], gs.at[at + k], gr.at[at + k], z_to[k])
        yield
        for k in range(1, 4):
            got(gz_recv.at[p, k - 1], gs.at[at + k], gr.at[at + k])

        def z_sum(t, _):
            rows = span(t * 64, 64)
            g_plane[p, rows] = (
                g_half[p, span(r * 256 + t * 64, 64)].astype(F32) + gz_recv[p, 0, rows].astype(F32)
                + gz_recv[p, 1, rows].astype(F32) + gz_recv[p, 2, rows].astype(F32)).astype(BF16)
            return 0

        lax.fori_loop(0, 4, z_sum, 0)

        def plane_out(q):
            return remote(
                g_plane.at[p, span(chunk_at(q), 16)], gp_recv.at[p, q - 1],
                gs.at[at + 3 + q], gr.at[at + 3 + q], peer_at(q))

        def begin(q, _):
            plane_out(q).start()
            return 0

        lax.fori_loop(1, 16, begin, 0)
        yield

        def plane_sum(q, held):
            plane_out(q).wait()
            return held + gp_recv[p, q - 1].astype(F32)

        held = lax.fori_loop(1, 16, plane_sum, g_plane[p, span(chunk_at(0), 16)].astype(F32))
        mine = span(base + r * 256 + chunk_at(0), 16)
        summed[p, mine] = held.astype(BF16)

        def back_out(q):
            return remote(whole.at[mine], whole.at[mine], gs.at[at + 18 + q], gr.at[at + 18 + q], peer_at(q))

        def begin_back(q, _):
            back_out(q).start()
            return 0

        lax.fori_loop(1, 16, begin_back, 0)
        yield

        def end_back(q, _):
            back_out(q).wait_send()
            there = whole.at[span(base + r * 256 + chunk_at(other_way(q)), 16)]
            remote(there, there, gs.at[at + 18 + q], gr.at[at + 18 + q], mate).wait_recv()
            return 0

        lax.fori_loop(1, 16, end_back, 0)
        line_part = whole.at[span(base + r * 256, 256)]
        for k in range(1, 4):
            send(line_part, line_part, gs.at[at + 33 + k], gr.at[at + 33 + k], z_to[k])
        yield
        for k, source in ((1, rk[2]), (2, rk[1]), (3, rk[3])):
            got(whole.at[span(base + source * 256, 256)], gs.at[at + 33 + k], gr.at[at + 33 + k])
        half = whole.at[span(base, 1024)]
        send(half, half, gs.at[at + 37], gr.at[at + 37], mate)
        yield
        got(whole.at[span(1024 - base, 1024)], gs.at[at + 37], gr.at[at + 37])
        yield

    states_in, first, second, ring = gather(), weights(0), weights(1), rings()
    next(states_in)
    own_rows()
    own_keys()
    plan_parts()
    next(states_in)
    far_keys()
    for _ in range(4):
        next(states_in)
    fetched_keys()
    lax.fori_loop(0, 4, attend, 0)
    tasks = {
        "Q": query_output, "K": key_value, "N": lambda: (near_parts(0), near_parts(1)), "E": edge_parts, "O": own_parts,
        "w": lambda: next(first), "v": lambda: next(second), "r": lambda: next(ring),
    }
    for step in PLAN:
        if step in "0123":
            exchange(int(step))
        else:
            tasks[step]()
    for copy in started:
        copy.wait_send()


AHEAD = 1
PLAN = "QwKvN3wv12r0wrrEOwvrrvwrrrvrwrwvv"


def layer(neighbours, states, gain, labels, wq, wk, wv, wo, cot):
    vmem = pl.BlockSpec(memory_space=pltpu.VMEM)
    smem = pl.BlockSpec(memory_space=pltpu.SMEM)
    anywhere = pl.BlockSpec(memory_space=pl.ANY)
    dma = pltpu.SemaphoreType.DMA

    def half(*shape):
        return pltpu.VMEM(shape, BF16)

    def full(*shape):
        return pltpu.VMEM(shape, F32)

    def whole(*shape):
        return pltpu.VMEM(shape, jnp.int32)

    return pl.pallas_call(
        layer_kernel,
        out_shape=(
            jax.ShapeDtypeStruct((256, 512), BF16),
            jax.ShapeDtypeStruct((256, 512), BF16),
            jax.ShapeDtypeStruct((2, 2048, 256), BF16),
        ),
        in_specs=[smem] + [vmem] * 3 + [anywhere] * 5,
        out_specs=[vmem] * 3,
        scratch_shapes=[
            half(512, 512), half(512, 512), half(512, 512), half(512, 512), half(256, 512),
            whole(8, 128), half(2, 4, 4, 2, 128, 512), whole(2, 4, 4, 8, 128), half(2, 128, 512), whole(8, 128),
            pltpu.SMEM((64,), jnp.int32),
            half(256, 512), half(256, 512), half(256, 512),
            half(2, 768, 512), half(2, 768, 512), half(2, 768, 512), full(2, 8, 768), full(2, 128, 768),
            half(512, 256), half(512, 256), full(512, 768), full(512, 768), half(512, 768), half(512, 768),
            half(256, 512), half(256, 512), half(2, 1024, 768),
            half(9, 512, 128), half(2, 512, 128), half(2, 512, 128), full(512, 256),
            half(16, 2, 512, 128), half(16, 2, 512, 128),
            half(4, 2, 512, 128), half(4, 2, 512, 128),
            half(4, 2, 2, 512, 128), half(4, 2, 2, 512, 128), half(4, 2, 512, 128),
            half(2, 512, 128), half(2, 2, 512, 128), half(2, 2, 512, 128), half(2, 512, 128), full(512, 256),
            half(2, 2048, 256), half(2, 1024, 256), half(2, 1024, 256), half(2, 3, 256, 256),
            half(2, 256, 256), half(2, 15, 16, 256),
            dma((5,)), dma((30,)), dma((30,)), dma((16,)), dma((16,)), dma((7,)), dma((7,)), dma((3,)), dma((3,)),
            dma((16,)), dma((16,)), dma((16,)), dma((16,)), dma((4,)), dma((4,)), dma((76,)), dma((76,)),
        ],
        compiler_params=pltpu.CompilerParams(collective_id=0, has_side_effects=True, vmem_limit_bytes=VMEM_LIMIT),
    )(neighbours, states, gain, labels, wq, wk, wv, wo, cot)


def finish_kernel(
    sum_query, sum_key, sum_value, sum_output, wq, wk, wv, gain, branch_in, states_in,
    branch, grad_states, grad_query, grad_key, grad_value, grad_output, grad_gain,
):
    branch[...] = branch_in[...]
    grad_states[...] = states_in[...]
    scale = 1.0 / math.sqrt(32768)
    along = jnp.zeros((128, 256), F32)
    for summed, weight, out in ((sum_query, wq, grad_query), (sum_key, wk, grad_key), (sum_value, wv, grad_value)):
        for half in range(2):
            cols = slice(half * 256, half * 256 + 256)
            value = summed[0, 0, half].astype(F32) * scale
            out[:, cols] = value
            along = along + value * weight[:, cols].astype(F32)
    for side in range(2):
        grad_output[:, side * 256 : side * 256 + 256] = sum_output[0, 0, side].astype(F32) * scale
    turned = (along[:, :128] + along[:, 128:]).T
    grad_gain[...] = jnp.sum(turned, axis=0, keepdims=True) / gain[...]


def finish(summed, wq, wk, wv, gain, branch, grad_states):
    square = jax.ShapeDtypeStruct((512, 512), F32)
    rows = jax.ShapeDtypeStruct((256, 512), BF16)
    by_row = pl.BlockSpec((128, 512), lambda i: (i, 0))
    thin = pl.BlockSpec((64, 512), lambda i: (i, 0))
    line = pl.BlockSpec((1, 128), lambda i: (0, i))

    def product(p, m):
        return pl.BlockSpec((1, 1, 2, 128, 256), lambda i: (p, m, 0, i, 0))

    by_product = summed.reshape(2, 2, 2, 512, 256)
    return pl.pallas_call(
        finish_kernel,
        grid=(4,),
        out_shape=(rows, rows, square, square, square, square, jax.ShapeDtypeStruct((1, 512), F32)),
        in_specs=[product(0, 0), product(1, 0), product(1, 1), product(0, 1), by_row, by_row, by_row, line, thin, thin],
        out_specs=[thin, thin, by_row, by_row, by_row, by_row, line],
        compiler_params=pltpu.CompilerParams(vmem_limit_bytes=VMEM_LIMIT),
    )(by_product, by_product, by_product, by_product, wq, wk, wv, gain, branch, grad_states)


def body(states, norm_gain, w_query, w_key, w_value, w_out, neighbours, labels, cotangent):
    gain = norm_gain.reshape(1, -1)
    branch_out, grad_states, summed = layer(
        neighbours, states.reshape(2, 128, 512), gain, labels, w_query, w_key, w_value, w_out, cotangent)
    outs = finish(summed, w_query, w_key, w_value, gain, branch_out, grad_states)
    return *outs[:6], outs[6].reshape(-1)


def solution(mesh):
    rows = P(("region", "dev"), None)
    return jax.shard_map(
        body, mesh=mesh,
        in_specs=(rows, P(), P(), P(), P(), P(), rows, rows, rows),
        out_specs=(rows, rows, P(), P(), P(), P(), P()),
        check_vma=False)
```

```python
import math

import jax
import jax.numpy as jnp
from jax import lax
from jax.experimental import pallas as pl
from jax.experimental.pallas import tpu as pltpu
from jax.sharding import PartitionSpec as P

MESH = pl.DeviceIdType.MESH
HEADS = 8
EPSILON = 1e-05
F32 = jnp.float32
BF16 = jnp.bfloat16
VMEM_LIMIT = 58 * 1024 * 1024
NN = (((1,), (0,)), ((), ()))
NT = (((1,), (1,)), ((), ()))
TN = (((0,), (0,)), ((), ()))


def dot(left, right, how=NN):
    return lax.dot_general(left, right, how, preferred_element_type=F32)


def place():
    r = lax.axis_index("region")
    d = lax.axis_index("dev")
    c = lax.rem(d, 2)
    x = lax.rem(lax.div(d, 2), 4)
    y = lax.div(d, 8)
    return r, c, x * (1 - c) + y * c, y * (1 - c) + x * c


def turn(value, step):
    return lax.rem(value + step + 4, 4)


def dev_at(a, b, c):
    return ((b * (1 - c) + a * c) * 4 + a * (1 - c) + b * c) * 2 + c


def around(value):
    return [value, turn(value, -1), turn(value, 1), turn(value, 2)]


def normalize(rows, gain):
    wide = rows.astype(F32)
    inverse = lax.rsqrt(jnp.mean(wide * wide, axis=-1, keepdims=True) + EPSILON)
    return (wide * inverse * gain).astype(BF16)


def remote(src, dst, s, q, to):
    return pltpu.make_async_remote_copy(
        src_ref=src, dst_ref=dst, send_sem=s, recv_sem=q, device_id=to, device_id_type=MESH)


def span(first, size):
    return pl.ds(pl.multiple_of(first, 16), size)


def layer_kernel(
    near_ref, states, gain, labels, wq_hbm, wk_hbm, wv_hbm, wo_hbm, cot_hbm,
    branch, grad_states, summed,
    wq, wk, wv, wo, cot, marks, g, gl, far, fl, table,
    normed, packed, q_own, d_att, keys, normed_keys, values, key_marks, bias,
    q_wide, d_wide, scores, d_probs, probs, d_scores, att, dq, kv_grad,
    parts, far_two, far_parts, base_t,
    give, take, far_send, far_recv, near_send, near_recv, line,
    far2_recv, near2_send, near2_recv, z_part, total,
    grads, g_mate, g_half, gz_recv, g_plane, gp_recv,
    load_s, as_, ar, mate_s, mate_r, ls, lr, zs, zr,
    give_s, take_s, s1s, s1r, s2s, s2r, gs, gr,
):
    r, c, a, b = place()
    d = lax.axis_index("dev")
    x, y = lax.rem(lax.div(d, 2), 4), lax.div(d, 8)
    ak, bk, rk = around(a), around(b), around(r)
    mate = (r, d + 1 - 2 * c)
    a_to = [(r, dev_at(k, b, c)) for k in ak]
    b_to = [(r, dev_at(a, k, c)) for k in bk]
    z_to = [(k, d) for k in rk]

    def peer_at(q):
        return (r, (turn(y, lax.div(q, 4)) * 4 + turn(x, lax.rem(q, 4))) * 2 + c)

    loads = []
    for n, (src, dst) in enumerate(((wq_hbm, wq), (cot_hbm, cot), (wo_hbm, wo), (wk_hbm, wk), (wv_hbm, wv))):
        load = pltpu.make_async_copy(src, dst, load_s.at[n])
        load.start()
        loads.append(load)
    barrier = pltpu.get_barrier_semaphore()
    for peer in [mate] + z_to[1:]:
        pl.semaphore_signal(barrier, inc=1, device_id=peer, device_id_type=MESH)

    def greet(q, _):
        pl.semaphore_signal(barrier, inc=1, device_id=peer_at(q), device_id_type=MESH)
        return 0

    lax.fori_loop(1, 16, greet, 0)
    marks[...] = jnp.zeros((8, 128), jnp.int32)
    marks[:2] = labels[...]
    gain_row = gain[...]
    for k in range(2):
        packed[k] = normalize(states[k], gain_row)
    pl.semaphore_wait(barrier, 19)
    started = []

    def send(src, dst, s, q, to):
        copy = remote(src, dst, s, q, to)
        copy.start()
        started.append(copy)

    def got(dst, s, q):
        remote(dst, dst, s, q, mate).wait_recv()

    def gather():
        def slot(i, j):
            return g.at[c, bk[j], ak[i]]

        def first_in(n, i, half):
            got(slot(i, 0).at[half], as_.at[n], ar.at[n])

        def out(n, src, dst, to):
            send(src, dst, as_.at[n], ar.at[n], to)

        def cross(i, j):
            src = packed if i == 0 and j == 0 else slot(i, j)
            send(src, slot(i, j), mate_s.at[i * 4 + j], mate_r.at[i * 4 + j], mate)

        def second_out(i, half, way):
            src = packed if i == 0 else slot(i, 0)
            out(6 + 6 * i + 2 * way + half, src.at[half], slot(i, 0).at[half], b_to[2 - way])

        def second_in(i, half, way):
            n = 6 + 6 * i + 2 * way + half
            got(slot(i, 1 + way).at[half], as_.at[n], ar.at[n])

        def second_on(i, way):
            second_in(i, way, way)
            there = slot(i, 1 + way).at[way]
            out(10 + 6 * i + way, there, there, b_to[2 - way])

        def first_on(way):
            first_in(2 * way + way, 1 + way, way)
            there = slot(1 + way, 0).at[way]
            out(4 + way, there, there, a_to[2 - way])

        for block in range(2):
            for way in range(2):
                half = block if way == 0 else 1 - block
                out(2 * way + half, packed.at[half], slot(0, 0).at[half], a_to[2 - way])
            for way in range(2):
                second_out(0, block if way == 0 else 1 - block, way)
        row = gl.at[c, b, a]
        send(marks, row, ls.at[0], lr.at[0], a_to[2])
        send(marks, row, ls.at[1], lr.at[1], a_to[1])
        send(packed, far, zs.at[0], zr.at[0], z_to[1])
        send(marks, fl, zs.at[1], zr.at[1], z_to[1])
        cross(0, 0)
        g[c, b, a] = packed[...]
        gl[c, b, a] = marks[...]
        yield
        for way in range(2):
            first_on(way)
            second_out(1 + way, way, way)
            second_out(1 + way, way, 1 - way)
        for way in range(2):
            second_on(0, way)
        for way in range(2):
            first_in(2 * way + 1 - way, 1 + way, 1 - way)
            second_out(1 + way, 1 - way, 1 - way)
            second_out(1 + way, 1 - way, way)
            cross(1 + way, 0)
        for way in range(2):
            second_in(0, 1 - way, way)
            cross(0, 1 + way)
        got(gl.at[c, b, ak[1]], ls.at[0], lr.at[0])
        send(gl.at[c, b, ak[1]], gl.at[c, b, ak[1]], ls.at[2], lr.at[2], a_to[2])
        got(gl.at[c, b, ak[2]], ls.at[1], lr.at[1])
        yield
        for way in range(2):
            got(slot(3, 0).at[way], as_.at[4 + way], ar.at[4 + way])
            second_out(3, way, way)
            second_out(3, way, 1 - way)
        cross(3, 0)
        got(gl.at[c, b, ak[3]], ls.at[2], lr.at[2])
        send(gl.at[c, b], gl.at[c, b], ls.at[3], lr.at[3], b_to[2])
        send(gl.at[c, b], gl.at[c, b], ls.at[4], lr.at[4], b_to[1])
        yield
        for way in range(2):
            second_on(1 + way, way)
        for way in range(2):
            second_on(2 - way, way)
        for i in (1, 2):
            for way in range(2):
                second_in(i, 1 - way, way)
                cross(i, 1 + way)
        yield
        got(gl.at[c, bk[1]], ls.at[3], lr.at[3])
        send(gl.at[c, bk[1]], gl.at[c, bk[1]], ls.at[5], lr.at[5], b_to[2])
        got(gl.at[c, bk[2]], ls.at[4], lr.at[4])
        for way in range(2):
            second_on(3, way)
        for way in range(2):
            second_in(3, 1 - way, way)
            cross(3, 1 + way)
        yield
        got(gl.at[c, bk[3]], ls.at[5], lr.at[5])
        send(gl.at[c], gl.at[c], ls.at[6], lr.at[6], mate)
        for i in range(4):
            for way in range(2):
                got(slot(i, 3).at[way], as_.at[10 + 6 * i + way], ar.at[10 + 6 * i + way])
            cross(i, 3)
        for i in range(4):
            for j in range(4):
                got(g.at[1 - c, ak[j], bk[i]], mate_s.at[i * 4 + j], mate_r.at[i * 4 + j])
        got(gl.at[1 - c], ls.at[6], lr.at[6])
        yield

    def own_rows():
        for n in range(3):
            loads[n].wait()
        for k in range(2):
            rows = slice(k * 128, (k + 1) * 128)
            normed[rows] = packed[k]
            normed_keys[k, :128] = normed[rows]
        q_own[...] = (dot(normed[...], wq[...]).astype(BF16) * 0.125).astype(BF16)
        d_att[...] = dot(cot[...], wo[...], NT).astype(BF16)

    def project(k, rows):
        n = normed_keys[k, rows]
        keys[k, rows] = dot(n, wk[...]).astype(BF16)
        values[k, rows] = dot(n, wv[...]).astype(BF16)

    def own_keys():
        for n in (3, 4):
            loads[n].wait()
        for k in range(2):
            project(k, slice(0, 128))
            key_marks[k, :, :128] = jnp.broadcast_to(marks[k : k + 1], (8, 128)).astype(F32)

    def far_keys():
        got(far, zs.at[0], zr.at[0])
        got(fl, zs.at[1], zr.at[1])
        for k in range(2):
            m = lax.rem(near_ref[k, 5], 2)
            normed_keys[k, 640:] = far[m]
            project(k, slice(640, 768))
            key_marks[k, :, 640:] = jnp.broadcast_to(fl[pl.ds(m, 1)], (8, 128)).astype(F32)

    def plan_parts():
        wanted = [lax.rem(near_ref[k, 1 + e], 64) for k in range(2) for e in range(4)]

        def look(t, _):
            found = jnp.int32(8)
            for n, block in enumerate(wanted):
                found = jnp.where(block == t, n, found)
            table[t] = found
            return 0

        lax.fori_loop(0, 64, look, 0)
        parts[8] = jnp.zeros((512, 128), BF16)

    def fetch(k, e):
        block = near_ref[k, 1 + e]
        at = lax.rem(lax.div(block, 2), 32)
        core = lax.rem(at, 2)
        ax = lax.rem(lax.div(at, 2), 4)
        ay = lax.div(at, 8)
        first, second = ax * (1 - core) + ay * core, ay * (1 - core) + ax * core
        local = lax.rem(block, 2)
        rows = slice((1 + e) * 128, (2 + e) * 128)
        normed_keys[k, rows] = g[core, second, first, local]
        key_marks[k, :, rows] = jnp.broadcast_to(gl[core, second, first, pl.ds(local, 1)], (8, 128)).astype(F32)

    def fetched_keys():
        for k in range(2):
            for e in range(4):
                fetch(k, e)
        for k in range(2):
            def one(e, _, k=k):
                project(k, span(128 + e * 256, 256))
                return 0

            lax.fori_loop(0, 2, one, 0)
        for k in range(2):
            own = jnp.broadcast_to(marks[k : k + 1], (128, 128)).astype(F32).T
            for e in range(6):
                at = slice(e * 128, (e + 1) * 128)
                gap = jnp.abs(own - jnp.broadcast_to(key_marks[k, :1, at], (128, 128)))
                bias[k, :, at] = jnp.where(gap <= 1.0, 0.0, -jnp.inf)

    head_of = lax.broadcasted_iota(jnp.int32, (128, 256), 1) // 64

    def widen():
        for n in range(4):
            rows, cols = slice(n // 2 * 128, n // 2 * 128 + 128), slice(n % 2 * 256, n % 2 * 256 + 256)
            q_part, d_part = q_own[rows, cols].astype(F32), d_att[rows, cols].astype(F32)
            for i in range(4):
                at = slice(i * 128, (i + 1) * 128)
                q_wide[n, at] = jnp.where(head_of == i, q_part, 0.0).astype(BF16)
                d_wide[n, at] = jnp.where(head_of == i, d_part, 0.0).astype(BF16)

    def attend(n, _):
        k, half = lax.div(n, 2), lax.rem(n, 2)
        rows = pl.ds(pl.multiple_of(k * 128, 128), 128)
        cols = pl.ds(pl.multiple_of(half * 256, 256), 256)
        scores[...] = dot(q_wide[n], keys[k, :, cols], NT)
        d_probs[...] = dot(d_wide[n], values[k, :, cols], NT)

        def soft(t, _):
            at = pl.ds(pl.multiple_of(t * 128, 128), 128)
            w = jnp.exp(scores[at] + bias[k])
            p = w * (1.0 / jnp.sum(w, axis=-1, keepdims=True))
            dp = d_probs[at]
            mean = jnp.sum(p * dp, axis=-1, keepdims=True)
            probs[at] = p.astype(BF16)
            d_scores[at] = (p * (dp - mean)).astype(BF16)
            return 0

        lax.fori_loop(0, 4, soft, 0, unroll=2)
        mixed = dot(probs[...], values[k, :, cols])
        turned = dot(d_scores[...], keys[k, :, cols])
        one = jnp.zeros((128, 256), F32)
        two = jnp.zeros((128, 256), F32)
        for i in range(4):
            at = slice(i * 128, (i + 1) * 128)
            one = one + jnp.where(head_of == i, mixed[at], 0.0)
            two = two + jnp.where(head_of == i, turned[at], 0.0)
        att[rows, cols] = one.astype(BF16)
        dq[rows, cols] = (two * 0.125).astype(BF16)
        kv_grad[k, cols] = dot(q_wide[n], d_scores[...], TN).astype(BF16)
        kv_grad[k, pl.ds(pl.multiple_of(512 + half * 256, 256), 256)] = dot(d_wide[n], probs[...], TN).astype(BF16)
        return 0

    def hold(p, m, value):
        for half in range(2):
            grads[p, pl.ds(m * 1024 + half * 512, 512)] = value[:, half * 256 : (half + 1) * 256].astype(BF16)

    def query_output():
        hold(0, 0, dot(normed[...], dq[...], TN))
        hold(0, 1, dot(att[...], cot[...], TN))

    def key_value():
        for m in range(2):
            at = slice(m * 512, (m + 1) * 512)
            hold(1, m, (dot(kv_grad[0, at], normed_keys[0]) + dot(kv_grad[1, at], normed_keys[1])).T)

    def part_of(k, at):
        return dot(wk[...], kv_grad[k, :512, at]) + dot(wv[...], kv_grad[k, 512:, at])

    def near_parts(k):
        for pair in range(2):
            value = part_of(k, slice(128 + pair * 256, 384 + pair * 256)).astype(BF16)
            for e in range(2):
                parts[k * 4 + pair * 2 + e] = value[:, e * 128 : (e + 1) * 128]

    def edge_parts():
        for k in range(2):
            far_two[k] = part_of(k, slice(640, 768)).astype(BF16)
        m = lax.rem(near_ref[0, 5], 2)
        for k in range(2):
            far_parts[k] = far_two[lax.rem(k + m, 2)]
        send(far_parts, z_part, zs.at[2], zr.at[2], z_to[2])

    def own_parts():
        mine = dot(wq[...], dq[...], NT)
        for k in range(2):
            at = slice(k * 128, (k + 1) * 128)
            base_t[:, at] = mine[:, at] + part_of(k, slice(0, 128)).astype(BF16).astype(F32)
        branch[...] = dot(att[...], wo[...]).astype(BF16)

    def each(work):
        def step(t, _):
            work(pl.ds(pl.multiple_of(t * 128, 128), 128))
            return 0

        lax.fori_loop(0, 4, step, 0)

    def here(i, j, block, rows):
        mine = parts[table[2 * dev_at(ak[i], bk[j], c) + block], rows]
        return mine.astype(F32) + take[i * 4 + j, block, rows].astype(F32)

    def took(i, j):
        got(take.at[i * 4 + j], give_s.at[i * 4 + j], take_s.at[i * 4 + j])

    order = (3, 1, 2, 0)

    def exchange(j):
        for i in order:
            n = i * 4 + j
            for block in range(2):
                give[n, block] = parts[table[2 * dev_at(bk[i], ak[j], 1 - c) + block]]
            send(give.at[n], take.at[n], give_s.at[n], take_s.at[n], mate)

    def rings():
        for i in order:
            took(i, 3)
            for block in range(2):
                def far_sum(rows, block=block, i=i):
                    far_send[i, block, rows] = here(i, 3, block, rows).astype(BF16)

                each(far_sum)
                send(far_send.at[i, block], far_recv.at[i, block], s1s.at[i * 4 + block], s1r.at[i * 4 + block], b_to[2 - block])
        yield
        near_copies = []
        for i in order:
            for way in range(2):
                j = 2 - way
                took(i, j)
                got(far_recv.at[i, way], s1s.at[i * 4 + way], s1r.at[i * 4 + way])

                def near_sum(rows, way=way, i=i, j=j):
                    near_send[i, way, way, rows] = (here(i, j, way, rows) + far_recv[i, way, rows].astype(F32)).astype(BF16)
                    near_send[i, way, 1 - way, rows] = here(i, j, 1 - way, rows).astype(BF16)

                each(near_sum)
                if len(near_copies) >= 2 * AHEAD:
                    near_copies[-2 * AHEAD].wait_send()
                copy = remote(near_send.at[i, way], near_recv.at[i, way], s1s.at[i * 4 + 2 + way], s1r.at[i * 4 + 2 + way], b_to[j])
                copy.start()
                near_copies.append(copy)
            yield
        started.extend(near_copies[-2 * AHEAD :])

        def ring_end(i):
            took(i, 0)
            for way in range(2):
                got(near_recv.at[i, way], s1s.at[i * 4 + 2 + way], s1r.at[i * 4 + 2 + way])
            for block in range(2):
                def end(rows, block=block):
                    line[i, block, rows] = (
                        here(i, 0, block, rows) + near_recv[i, 0, block, rows].astype(F32)
                        + near_recv[i, 1, block, rows].astype(F32)).astype(BF16)

                each(end)

        ring_end(3)
        for block in range(2):
            send(line.at[3, block], far2_recv.at[block], s2s.at[block], s2r.at[block], a_to[2 - block])
        yield
        for way in (1, 0):
            ring_end(2 - way)
            got(far2_recv.at[way], s2s.at[way], s2r.at[way])

            def near2(rows, way=way):
                near2_send[way, way, rows] = (line[2 - way, way, rows].astype(F32) + far2_recv[way, rows].astype(F32)).astype(BF16)
                near2_send[way, 1 - way, rows] = line[2 - way, 1 - way, rows]

            each(near2)
            send(near2_send.at[way], near2_recv.at[way], s2s.at[2 + way], s2r.at[2 + way], a_to[2 - way])
            yield
        ring_end(0)
        yield
        for way in range(2):
            got(near2_recv.at[way], s2s.at[2 + way], s2r.at[2 + way])
        got(z_part, zs.at[2], zr.at[2])
        for block in range(2):
            def last(rows, block=block):
                at = slice(block * 128, block * 128 + 128)
                total[rows, at] = (
                    base_t[rows, at] + line[0, block, rows].astype(F32) + near2_recv[0, block, rows].astype(F32)
                    + near2_recv[1, block, rows].astype(F32) + z_part[block, rows].astype(F32))

            each(last)
        for block in range(2):
            rows = slice(block * 128, block * 128 + 128)
            d_normed = total[:, rows].T
            wide = states[block].astype(F32)
            inverse = lax.rsqrt(jnp.mean(wide * wide, axis=-1, keepdims=True) + EPSILON)
            scaled = d_normed * gain_row
            along = jnp.sum(scaled * wide, axis=-1, keepdims=True) * (1.0 / 512)
            grad_states[rows] = (inverse * scaled - wide * (inverse * inverse * inverse * along)).astype(BF16)
        yield

    base = c * 1024

    def chunk_at(q):
        return (turn(y, lax.div(q, 4)) * 4 + turn(x, lax.rem(q, 4))) * 16

    def other_way(q):
        return lax.rem(4 - lax.div(q, 4), 4) * 4 + lax.rem(4 - lax.rem(q, 4), 4)

    def weights(p):
        at = p * 38
        whole = summed.at[p]
        send(grads.at[p, span(1024 - base, 1024)], g_mate.at[p], gs.at[at], gr.at[at], mate)
        yield
        got(g_mate.at[p], gs.at[at], gr.at[at])

        def half_sum(t, _):
            rows = span(t * 128, 128)
            g_half[p, rows] = (grads[p, span(base + t * 128, 128)].astype(F32) + g_mate[p, rows].astype(F32)).astype(BF16)
            return 0

        lax.fori_loop(0, 8, half_sum, 0)
        for k in range(1, 4):
            send(g_half.at[p, span(rk[k] * 256, 256)], gz_recv.at[p, k - 1], gs.at[at + k], gr.at[at + k], z_to[k])
        yield
        for k in range(1, 4):
            got(gz_recv.at[p, k - 1], gs.at[at + k], gr.at[at + k])

        def z_sum(t, _):
            rows = span(t * 64, 64)
            g_plane[p, rows] = (
                g_half[p, span(r * 256 + t * 64, 64)].astype(F32) + gz_recv[p, 0, rows].astype(F32)
                + gz_recv[p, 1, rows].astype(F32) + gz_recv[p, 2, rows].astype(F32)).astype(BF16)
            return 0

        lax.fori_loop(0, 4, z_sum, 0)

        def plane_out(q):
            return remote(
                g_plane.at[p, span(chunk_at(q), 16)], gp_recv.at[p, q - 1],
                gs.at[at + 3 + q], gr.at[at + 3 + q], peer_at(q))

        def begin(q, _):
            plane_out(q).start()
            return 0

        lax.fori_loop(1, 16, begin, 0)
        yield

        def plane_sum(q, held):
            plane_out(q).wait()
            return held + gp_recv[p, q - 1].astype(F32)

        held = lax.fori_loop(1, 16, plane_sum, g_plane[p, span(chunk_at(0), 16)].astype(F32))
        mine = span(base + r * 256 + chunk_at(0), 16)
        summed[p, mine] = held.astype(BF16)

        def back_out(q):
            return remote(whole.at[mine], whole.at[mine], gs.at[at + 18 + q], gr.at[at + 18 + q], peer_at(q))

        def begin_back(q, _):
            back_out(q).start()
            return 0

        lax.fori_loop(1, 16, begin_back, 0)
        yield

        def end_back(q, _):
            back_out(q).wait_send()
            there = whole.at[span(base + r * 256 + chunk_at(other_way(q)), 16)]
            remote(there, there, gs.at[at + 18 + q], gr.at[at + 18 + q], mate).wait_recv()
            return 0

        lax.fori_loop(1, 16, end_back, 0)
        line_part = whole.at[span(base + r * 256, 256)]
        for k in range(1, 4):
            send(line_part, line_part, gs.at[at + 33 + k], gr.at[at + 33 + k], z_to[k])
        yield
        for k, source in ((1, rk[2]), (2, rk[1]), (3, rk[3])):
            got(whole.at[span(base + source * 256, 256)], gs.at[at + 33 + k], gr.at[at + 33 + k])
        half = whole.at[span(base, 1024)]
        send(half, half, gs.at[at + 37], gr.at[at + 37], mate)
        yield
        got(whole.at[span(1024 - base, 1024)], gs.at[at + 37], gr.at[at + 37])
        yield

    states_in, first, second, ring = gather(), weights(0), weights(1), rings()
    next(states_in)
    own_rows()
    own_keys()
    plan_parts()
    next(states_in)
    far_keys()
    widen()
    for _ in range(4):
        next(states_in)
    fetched_keys()
    lax.fori_loop(0, 4, attend, 0)
    tasks = {
        "Q": query_output, "K": key_value, "N": lambda: (near_parts(0), near_parts(1)), "E": edge_parts, "O": own_parts,
        "w": lambda: next(first), "v": lambda: next(second), "r": lambda: next(ring),
    }
    for step in PLAN:
        if step in "0123":
            exchange(int(step))
        else:
            tasks[step]()
    for copy in started:
        copy.wait_send()


AHEAD = 1
PLAN = "QwKvwN3v12r0wrrEwvrrOvwrrrvrwrwvv"


def layer(neighbours, states, gain, labels, wq, wk, wv, wo, cot):
    vmem = pl.BlockSpec(memory_space=pltpu.VMEM)
    smem = pl.BlockSpec(memory_space=pltpu.SMEM)
    anywhere = pl.BlockSpec(memory_space=pl.ANY)
    dma = pltpu.SemaphoreType.DMA

    def half(*shape):
        return pltpu.VMEM(shape, BF16)

    def full(*shape):
        return pltpu.VMEM(shape, F32)

    def whole(*shape):
        return pltpu.VMEM(shape, jnp.int32)

    return pl.pallas_call(
        layer_kernel,
        out_shape=(
            jax.ShapeDtypeStruct((256, 512), BF16),
            jax.ShapeDtypeStruct((256, 512), BF16),
            jax.ShapeDtypeStruct((2, 2048, 256), BF16),
        ),
        in_specs=[smem] + [vmem] * 3 + [anywhere] * 5,
        out_specs=[vmem] * 3,
        scratch_shapes=[
            half(512, 512), half(512, 512), half(512, 512), half(512, 512), half(256, 512),
            whole(8, 128), half(2, 4, 4, 2, 128, 512), whole(2, 4, 4, 8, 128), half(2, 128, 512), whole(8, 128),
            pltpu.SMEM((64,), jnp.int32),
            half(256, 512), half(2, 128, 512), half(256, 512), half(256, 512),
            half(2, 768, 512), half(2, 768, 512), half(2, 768, 512), full(2, 8, 768), full(2, 128, 768),
            half(4, 512, 256), half(4, 512, 256), full(512, 768), full(512, 768), half(512, 768), half(512, 768),
            half(256, 512), half(256, 512), half(2, 1024, 768),
            half(9, 512, 128), half(2, 512, 128), half(2, 512, 128), full(512, 256),
            half(16, 2, 512, 128), half(16, 2, 512, 128),
            half(4, 2, 512, 128), half(4, 2, 512, 128),
            half(4, 2, 2, 512, 128), half(4, 2, 2, 512, 128), half(4, 2, 512, 128),
            half(2, 512, 128), half(2, 2, 512, 128), half(2, 2, 512, 128), half(2, 512, 128), full(512, 256),
            half(2, 2048, 256), half(2, 1024, 256), half(2, 1024, 256), half(2, 3, 256, 256),
            half(2, 256, 256), half(2, 15, 16, 256),
            dma((5,)), dma((30,)), dma((30,)), dma((16,)), dma((16,)), dma((7,)), dma((7,)), dma((3,)), dma((3,)),
            dma((16,)), dma((16,)), dma((16,)), dma((16,)), dma((4,)), dma((4,)), dma((76,)), dma((76,)),
        ],
        compiler_params=pltpu.CompilerParams(collective_id=0, has_side_effects=True, vmem_limit_bytes=VMEM_LIMIT),
    )(neighbours, states, gain, labels, wq, wk, wv, wo, cot)


def finish_kernel(
    sum_query, sum_key, sum_value, sum_output, wq, wk, wv, gain, branch_in, states_in,
    branch, grad_states, grad_query, grad_key, grad_value, grad_output, grad_gain,
):
    branch[...] = branch_in[...]
    grad_states[...] = states_in[...]
    scale = 1.0 / math.sqrt(32768)
    along = jnp.zeros((128, 256), F32)
    for summed, weight, out in ((sum_query, wq, grad_query), (sum_key, wk, grad_key), (sum_value, wv, grad_value)):
        for half in range(2):
            cols = slice(half * 256, half * 256 + 256)
            value = summed[0, 0, half].astype(F32) * scale
            out[:, cols] = value
            along = along + value * weight[:, cols].astype(F32)
    for side in range(2):
        grad_output[:, side * 256 : side * 256 + 256] = sum_output[0, 0, side].astype(F32) * scale
    turned = (along[:, :128] + along[:, 128:]).T
    grad_gain[...] = jnp.sum(turned, axis=0, keepdims=True) / gain[...]


def finish(summed, wq, wk, wv, gain, branch, grad_states):
    square = jax.ShapeDtypeStruct((512, 512), F32)
    rows = jax.ShapeDtypeStruct((256, 512), BF16)
    by_row = pl.BlockSpec((128, 512), lambda i: (i, 0))
    thin = pl.BlockSpec((64, 512), lambda i: (i, 0))
    line = pl.BlockSpec((1, 128), lambda i: (0, i))

    def product(p, m):
        return pl.BlockSpec((1, 1, 2, 128, 256), lambda i: (p, m, 0, i, 0))

    by_product = summed.reshape(2, 2, 2, 512, 256)
    return pl.pallas_call(
        finish_kernel,
        grid=(4,),
        out_shape=(rows, rows, square, square, square, square, jax.ShapeDtypeStruct((1, 512), F32)),
        in_specs=[product(0, 0), product(1, 0), product(1, 1), product(0, 1), by_row, by_row, by_row, line, thin, thin],
        out_specs=[thin, thin, by_row, by_row, by_row, by_row, line],
        compiler_params=pltpu.CompilerParams(vmem_limit_bytes=VMEM_LIMIT),
    )(by_product, by_product, by_product, by_product, wq, wk, wv, gain, branch, grad_states)


def body(states, norm_gain, w_query, w_key, w_value, w_out, neighbours, labels, cotangent):
    gain = norm_gain.reshape(1, -1)
    branch_out, grad_states, summed = layer(
        neighbours, states.reshape(2, 128, 512), gain, labels, w_query, w_key, w_value, w_out, cotangent)
    outs = finish(summed, w_query, w_key, w_value, gain, branch_out, grad_states)
    return *outs[:6], outs[6].reshape(-1)


def solution(mesh):
    rows = P(("region", "dev"), None)
    return jax.shard_map(
        body, mesh=mesh,
        in_specs=(rows, P(), P(), P(), P(), P(), rows, rows, rows),
        out_specs=(rows, rows, P(), P(), P(), P(), P()),
        check_vma=False)
```
